512 devices in a mesh: hour: 64 (over z_hi, y, core), bus: 8 (over x, z_lo).
Axes of the slice: x: 4, y: 8, z: 8 (z_hi: 4, z_lo: 2; z = z_hi * 2 + z_lo), core: 2. Of those that a mesh axis runs over, the one named last changes fastest.
Arguments:
- line_sensitivity: float32 [2000, 3072], P('bus'), may hold values from -0.125 to 0.125
- demand: float32 [2000, 8192], P('bus', 'hour'), may hold values from 0.05 to 1
- unit_cost: float32 [2000, 8192], P('bus', 'hour'), may hold values from 0.1 to 2
- output_limit: float32 [2000], P('bus'), may hold values from 0.2 to 2
- output_start: float32 [2000, 8192], P('bus', 'hour'), may hold values from 0 to 1
- line_limit: float32 [3072], replicated, may hold values from 0.1 to 1
- line_dual: float32 [3072, 8192], P('bus', 'hour'), may hold values from -3 to 3
- storage_bus: int32 [2000], P('bus'), may hold values from 0 to 1999, as said below
- charge_limit: float32 [2000], P('bus'), may hold values from 0.05 to 0.5
- charge_start: float32 [2000, 8192], P('bus', 'hour'), may hold values from -0.2 to 0.2
- level_start: float32 [2000], P('bus'), may hold values from 1 to 6
- level_limit: float32 [2000], P('bus'), may hold values from 3 to 30
- level_dual: float32 [2000, 8192], P('bus', 'hour'), may hold values from -0.2 to 0.2
- balance_dual: float32 [8192], P('hour'), may hold values from -3 to 3
Outputs:
- generation: float32 [2000, 8192], P('bus', 'hour')
- charging: float32 [2000, 8192], P('bus', 'hour')
- storage_level: float32 [2000, 8192], P('bus', 'hour')
- line_dual_next: float32 [3072, 8192], P('bus', 'hour')
- level_dual_next: float32 [2000, 8192], P('bus', 'hour')
- balance_dual_next: float32 [8192], P('hour')
The draws below stay inside these ranges and needn't reach their ends.
Inputs may be any that keep to these rules, and one draw needn't show every extreme that they name: `storage_bus`: storage s is connected to a bus b with b // 250 equal to s // 250; storage 0 is at bus 0 and storage 2000 - 1 at bus 2000 - 1.
All inputs are finite; a program needn't handle non-finite values.
Results may differ from the reference program's by a relative error of at most 0.00011.
Values sent between devices are 32-bit elements; how exact they have to be, the bound alone decides.
A program may use at most 64 MiB of HBM per device.

```python
import math
import jax
import jax.numpy as jnp
from jax import lax

B = 2000
L = 3072
S = 2000
ITERS = 2
HOURS = 8192
B_DEV = 250
S_DEV = 250


def draw_storage_bus(key, part):
    key = jax.random.fold_in(key, 11)
    index = jnp.arange(S)
    offset = jax.random.randint(key, (S,), 0, B_DEV)
    placed = index // S_DEV * B_DEV + offset
    placed = jnp.where(index == 0, 0, placed)
    placed = jnp.where(index == S - 1, B - 1, placed)
    return placed.astype(jnp.int32)


def block_scale(own_key, extent, pieces, least, high):
    def one(axis_at, blocks):
        steps = jax.random.uniform(jax.random.fold_in(jax.random.fold_in(own_key, 6), axis_at), (blocks,), jnp.float32, least / len(pieces), high / len(pieces))
        return jnp.repeat(jnp.exp(steps), extent[axis_at] // blocks).reshape((-1,) + (1,) * (len(extent) - axis_at - 1))

    loudness = one(*pieces[0])
    for cut in pieces[1:]:
        loudness = loudness * one(*cut)
    return loudness


def scatter_about(rng, dims, width, most, shards=(), held_as=jnp.bfloat16):
    drawn = width * jax.random.normal(rng, dims, jnp.float32)
    if shards:
        drawn = drawn * block_scale(rng, dims, shards, -0.22, 0.18)
    return jnp.clip(drawn, -most, most).astype(held_as)


def setup_inputs(seed: int = 0) -> dict:
    key_list = jax.random.split(jax.random.key(seed), 15)
    return {
        "line_sensitivity": scatter_about(key_list[0], (B, L), B ** -0.5, 0.125, ((0, 8),), jnp.float32),
        "demand": jnp.clip(jnp.exp(math.log(1.0) - 2.9957323 * jax.random.uniform(key_list[1], (B, HOURS), jnp.float32) ** block_scale(key_list[1], (B, HOURS), ((0, 8), (1, 64)), -0.2, 0.2)), 0.05, 1.0),
        "unit_cost": jnp.clip(jnp.exp(math.log(2.0) - 2.9957323 * jax.random.uniform(key_list[2], (B, HOURS), jnp.float32) ** block_scale(key_list[2], (B, HOURS), ((0, 8), (1, 64)), -0.2, 0.2)), 0.1, 2.0),
        "output_limit": jnp.clip(jnp.exp(math.log(2.0) - 2.3025851 * jax.random.uniform(key_list[3], (B,), jnp.float32) ** block_scale(key_list[3], (B,), ((0, 8),), -0.2, 0.2)), 0.2, 2.0),
        "output_start": jnp.clip(1.0 * jax.random.uniform(key_list[4], (B, HOURS), jnp.float32) ** block_scale(key_list[4], (B, HOURS), ((0, 8), (1, 64)), -0.2, 0.2), 0.0, 1.0),
        "line_limit": jnp.clip(jnp.exp(jax.random.uniform(key_list[5], (L,), jnp.float32, math.log(0.1), math.log(1.0))), 0.1, 1.0),
        "line_dual": scatter_about(key_list[6], (L, HOURS), 0.5, 3.0, ((0, 8), (1, 64)), jnp.float32),
        "storage_bus": draw_storage_bus(jax.random.fold_in(key_list[14], 71), 0),
        "charge_limit": jnp.clip(jnp.exp(math.log(0.5) - 2.3025851 * jax.random.uniform(key_list[8], (S,), jnp.float32) ** block_scale(key_list[8], (S,), ((0, 8),), -0.2, 0.2)), 0.05, 0.5),
        "charge_start": jnp.clip(jax.random.uniform(key_list[9], (S, HOURS), jnp.float32, -0.2, 0.2) * block_scale(key_list[9], (S, HOURS), ((0, 8), (1, 64)), -0.4, 0.0), -0.2, 0.2),
        "level_start": jnp.clip(1.0 + 5.0 * jax.random.uniform(key_list[10], (S,), jnp.float32) ** block_scale(key_list[10], (S,), ((0, 8),), -0.2, 0.2), 1.0, 6.0),
        "level_limit": jnp.clip(jnp.exp(math.log(30.0) - 2.3025851 * jax.random.uniform(key_list[11], (S,), jnp.float32) ** block_scale(key_list[11], (S,), ((0, 8),), -0.2, 0.2)), 3.0, 30.0),
        "level_dual": jnp.clip(jax.random.uniform(key_list[12], (S, HOURS), jnp.float32, -0.2, 0.2) * block_scale(key_list[12], (S, HOURS), ((0, 8), (1, 64)), -0.4, 0.0), -0.2, 0.2),
        "balance_dual": scatter_about(key_list[13], (HOURS,), 0.5, 3.0, ((0, 64),), jnp.float32),
    }


def reference(line_sensitivity, demand, unit_cost, output_limit, output_start, line_limit, line_dual, storage_bus, charge_limit, charge_start, level_start, level_limit, level_dual, balance_dual):
    hour_pos = jnp.arange(HOURS).astype(jnp.float32)
    step_charge = 1.0 / (HOURS - hour_pos + 4.0)
    generation = output_start
    charging = charge_start
    line_now = line_dual
    level_now = level_dual
    balance_now = balance_dual
    storage_level = jnp.zeros_like(charge_start)
    for iteration in range(ITERS):
        adjoint = jnp.dot(line_sensitivity, line_now, precision=lax.Precision.HIGHEST, preferred_element_type=jnp.float32)
        later = jnp.flip(jnp.cumsum(jnp.flip(level_now, 1), axis=1), 1)
        output_new = jnp.clip(generation - 0.25 * (unit_cost + adjoint + balance_now[None, :]), 0.0, output_limit[:, None])
        charge_grad = later - jnp.take(adjoint, storage_bus, axis=0) - balance_now[None, :]
        charge_new = jnp.clip(charging - step_charge[None, :] * charge_grad, -charge_limit[:, None], charge_limit[:, None])
        output_bar = 2.0 * output_new - generation
        charge_bar = 2.0 * charge_new - charging
        injection = output_bar - demand - jax.ops.segment_sum(charge_bar, storage_bus, num_segments=B)
        flows = lax.dot_general(line_sensitivity, injection, (((0,), (0,)), ((), ())), precision=lax.Precision.HIGHEST, preferred_element_type=jnp.float32)
        balance = jnp.sum(injection, axis=0)
        storage_level = level_start[:, None] + jnp.cumsum(charge_bar, axis=1)
        raised = 4.0 * line_now + flows
        line_now = 0.25 * (raised - jnp.clip(raised, -line_limit[:, None], line_limit[:, None]))
        raised_level = 4.0 * level_now + storage_level
        level_now = 0.25 * (raised_level - jnp.clip(raised_level, 0.0, level_limit[:, None]))
        balance_now = balance_now + balance / float(B + S)
        generation = output_new
        charging = charge_new
    return generation, charging, storage_level, line_now, level_now, balance_now
```

```python
import jax
import jax.numpy as jnp
from jax import lax
from jax.experimental import pallas as pl
from jax.experimental.pallas import tpu as pltpu
from jax.sharding import PartitionSpec as P

B = 2000
S = 2000
ITERS = 2
HOURS = 8192
NB = 250
NP = 256
HD = 128
LD = 384
NL = 3072
NX = 4
GROUP = 8
ROW = 8
MESH = pl.DeviceIdType.MESH
HIGHEST = lax.Precision.HIGHEST
F32 = jnp.float32
BF16 = jnp.bfloat16
PEERS = ((2, 1), (1, 1), (3, 1), (2, 0), (1, 0), (3, 0), (0, 1))
ARRAYS = 14


def dot(a, b, dims, precision=None):
    return lax.dot_general(a, b, (dims, ((), ())), precision=precision, preferred_element_type=F32)


def halves(value):
    high = value.astype(BF16)
    return high, (value - high.astype(F32)).astype(BF16)


class Place:
    def __init__(self):
        self.hour = lax.axis_index("hour")
        self.bus = lax.axis_index("bus")
        self.x = self.bus // 2
        self.z = lax.rem(self.bus, 2)
        self.member = lax.rem(self.hour, GROUP)
        self.group = self.hour // GROUP

    def block(self, dx, dz):
        return lax.rem(self.x + dx + NX, NX) * 2 + lax.rem(self.z + dz, 2)

    def bus_peer(self, dx, dz):
        return (self.hour, self.block(dx, dz))

    def member_peer(self, d):
        return (self.group * GROUP + lax.rem(self.member + d, GROUP), self.bus)

    def group_peer(self, d):
        return (lax.rem(self.group + d, GROUP) * GROUP + self.member, self.bus)


class Sends:
    def __init__(self):
        self.all = []

    def start(self, src, dst, send_sem, recv_sem, device):
        copy = pltpu.make_async_remote_copy(
            src_ref=src, dst_ref=dst, send_sem=send_sem, recv_sem=recv_sem, device_id=device, device_id_type=MESH
        )
        copy.start()
        self.all.append(copy)

    def finish(self):
        for copy in self.all:
            copy.wait_send()


def arrived(ref, send_sem, recv_sem, device):
    pltpu.make_async_remote_copy(
        src_ref=ref, dst_ref=ref, send_sem=send_sem, recv_sem=recv_sem, device_id=device, device_id_type=MESH
    ).wait_recv()


class Gather:
    def __init__(self, place, sends, buf, rows, cut, send_sem, recv_sem):
        h = rows // 2
        self.place, self.sends, self.buf = place, sends, buf
        self.send_sem, self.recv_sem = send_sem, recv_sem
        right, left, across = (1, 0), (3, 0), (0, 1)
        self.plan = {
            "r1": (right, (0, 0), 0, h),
            "r2": (right, (0, 0), h, rows),
            "r3": (right, (3, 0), 0, h),
            "r4": (right, (0, 1), cut, rows),
            "r5": (right, (3, 1), 0, h),
            "l1": (left, (0, 0), h, rows),
            "l2": (left, (0, 0), 0, h),
            "l3": (left, (1, 0), h, rows),
            "l4": (left, (0, 1), 0, rows - cut),
            "l5": (left, (1, 1), h, rows),
            "z1": (across, (0, 0), 0, h),
            "z2": (across, (0, 0), h, rows),
            "z3": (across, (3, 0), 0, h),
            "z4": (across, (1, 0), h, rows),
            "z5": (across, (3, 0), h, cut),
            "z6": (across, (1, 0), rows - cut, h),
        }
        self.number = {key: i for i, key in enumerate(self.plan)}

    def send(self, *keys):
        for key in keys:
            to, block, first, last = self.plan[key]
            ref = self.buf.at[self.place.block(*block), pl.ds(first, last - first)]
            i = self.number[key]
            self.sends.start(ref, ref, self.send_sem.at[i], self.recv_sem.at[i], self.place.bus_peer(*to))

    def wait(self, *keys):
        for key in keys:
            to, block, first, last = self.plan[key]
            at = self.place.block((block[0] - to[0]) % NX, (block[1] + to[1]) % 2)
            ref = self.buf.at[at, pl.ds(first, last - first)]
            i = self.number[key]
            arrived(ref, self.send_sem.at[i], self.recv_sem.at[i], self.place.bus_peer(*to))

    def begin(self):
        self.send("r1", "l1", "z1", "r2", "l2", "z2")

    def run(self, use):
        block = self.place.block
        use(block(0, 0))
        self.wait("r1")
        self.send("r3", "z3")
        self.wait("l1")
        self.send("l3", "z4")
        self.wait("r2")
        self.send("z5")
        self.wait("l2")
        self.send("z6")
        self.wait("z1")
        self.send("l4")
        self.wait("z2")
        self.send("r4")
        use(block(3, 0))
        self.wait("z3")
        self.send("r5")
        self.wait("z4")
        self.send("l5")
        use(block(1, 0))
        use(block(0, 1))
        self.wait("r3", "l3")
        use(block(2, 0))
        self.wait("z5", "r4")
        use(block(3, 1))
        self.wait("z6", "l4")
        use(block(1, 1))
        self.wait("r5", "l5")
        use(block(2, 1))


class Prefix:
    def __init__(self, place, sends, buf, send_sem, recv_sem):
        self.place, self.sends, self.buf = place, sends, buf
        self.send_sem, self.recv_sem = send_sem, recv_sem

    def begin(self, value):
        place = self.place
        self.buf[place.member] = dot(jnp.ones((ROW, HD), F32), value, ((1,), (1,)), HIGHEST)
        for d in range(1, GROUP):
            ref = self.buf.at[place.member]
            self.sends.start(ref, ref, self.send_sem.at[d - 1], self.recv_sem.at[d - 1], place.member_peer(d))

    def middle(self):
        place = self.place
        for d in range(1, GROUP):
            ref = self.buf.at[lax.rem(place.member - d + GROUP, GROUP)]
            arrived(ref, self.send_sem.at[d - 1], self.recv_sem.at[d - 1], place.member_peer(d))
        total = self.buf[0]
        for i in range(1, GROUP):
            total = total + self.buf[i]
        self.buf[GROUP + place.group] = total
        for d in range(1, GROUP):
            ref = self.buf.at[GROUP + place.group]
            i = GROUP - 2 + d
            self.sends.start(ref, ref, self.send_sem.at[i], self.recv_sem.at[i], place.group_peer(d))

    def end(self, reverse):
        place = self.place
        for d in range(1, GROUP):
            ref = self.buf.at[GROUP + lax.rem(place.group - d + GROUP, GROUP)]
            i = GROUP - 2 + d
            arrived(ref, self.send_sem.at[i], self.recv_sem.at[i], place.group_peer(d))
        count = 2 * GROUP * ROW
        row = lax.broadcasted_iota(jnp.int32, (count, HD), 0)
        slot = row // ROW
        first = lax.rem(row, ROW) == 0
        mine = jnp.where(slot < GROUP, place.member, place.group + GROUP)
        reached = (slot > mine) if reverse else (slot < mine)
        reached = reached & ((slot < GROUP) == (mine < GROUP)) & first
        gathered = self.buf[...].reshape(count, NP)
        return dot(gathered, reached.astype(F32), ((0,), (0,)), HIGHEST)[0:NB]


def kernel(*refs):
    (sens_h, demand_h, cost_h, olim_h, gen_h, llim_h, line_h, sbus_h, clim_h, chg_h, lstart_h, llev_h, ldual_h, bal_h) = refs[:14]
    (gen_o, chg_o, level_o, line_o, ldual_o, bal_o) = refs[14:20]
    (sens, demand, cost, olim_r, gen, llim_r, sbus_r, clim_r, chg, lstart_r, llev_r, ldual, bal, line0) = refs[20:34]
    (shi, slo, tail, lines1, lines2, part1, part2, recv1, recv2, acc, pad_l, pad_c, pad_i, hot, level_v, line_v, pre) = refs[34:51]
    (in_sem, out_sem, g1s, g1r, g2s, g2r, s1s, s1r, s2s, s2r, ps, pr) = refs[51:]
    place = Place()
    sends = Sends()

    ins = {}
    for i, (src, dst) in enumerate(
        (
            (line_h, line0),
            (ldual_h, ldual),
            (sens_h, sens),
            (llim_h, llim_r),
            (sbus_h, sbus_r),
            (olim_h, olim_r),
            (clim_h, clim_r),
            (lstart_h, lstart_r),
            (llev_h, llev_r),
            (bal_h, bal),
            (demand_h, demand),
            (cost_h, cost),
            (gen_h, gen),
            (chg_h, chg),
        )
    ):
        ins[i] = pltpu.make_async_copy(src, dst, in_sem.at[i])
        ins[i].start()

    barrier = pltpu.get_barrier_semaphore()
    partners = [place.bus_peer(*d) for d in PEERS]
    partners += [place.member_peer(d) for d in range(1, GROUP)]
    partners += [place.group_peer(d) for d in range(1, GROUP)]
    for device in partners:
        pl.semaphore_signal(barrier, inc=1, device_id=device, device_id_type=MESH)

    zeros = jnp.zeros((NP - NB, HD), F32)
    for ref in (pad_l, pad_c, pad_i):
        ref[NB:NP, :] = zeros
    acc[...] = jnp.zeros((NP, HD), F32)
    ins[0].wait()
    lines1[place.bus] = line0[...]
    pl.semaphore_wait(barrier, len(partners))

    gather1 = Gather(place, sends, lines1, LD, 256, g1s, g1r)
    gather1.begin()
    prefixes = [Prefix(place, sends, pre.at[k], ps.at[k], pr.at[k]) for k in range(4)]
    ins[1].wait()
    pad_l[0:NB, :] = ldual[...]
    prefixes[0].begin(pad_l[...])

    ins[2].wait()
    tail[0:10, :] = sens[240:NB, :]
    tail[10:16, :] = jnp.zeros((6, NL), F32)

    @pl.loop(0, 15)
    def _(i):
        rows = pl.ds(pl.multiple_of(i * 16, 16), 16)
        shi[rows, :], slo[rows, :] = halves(sens[rows, :])

    shi[240:NP, :], slo[240:NP, :] = halves(tail[...])

    for i in range(3, ARRAYS):
        ins[i].wait()

    def column(row, count):
        return jnp.broadcast_to(row, (HD, count)).T

    olim = column(olim_r[0:1, :], NB)
    clim = column(clim_r[0:1, :], NB)
    lstart = column(lstart_r[0:1, :], NB)
    llev = column(llev_r[0:1, :], NB)
    first_line = pl.multiple_of(place.bus * LD, HD)
    llim = column(llim_r[0:1, pl.ds(first_line, LD)], LD)
    at_bus = lax.broadcasted_iota(jnp.int32, (NP, NB), 0)
    local = sbus_r[0:1, :] - place.bus * NB
    hot[...] = jnp.zeros((NP, NP), F32)
    hot[:, 0:NB] = (at_bus == local).astype(F32)
    hour_at = lax.broadcasted_iota(jnp.int32, (HD, HD), 0)
    hour_to = lax.broadcasted_iota(jnp.int32, (HD, HD), 1)
    until = (hour_at <= hour_to).astype(F32)
    since = (hour_at >= hour_to).astype(F32)
    hour_pos = (place.hour * HD + lax.broadcasted_iota(jnp.int32, (1, HD), 1)).astype(F32)
    step = 1.0 / (float(HOURS) - hour_pos + 4.0)
    prefixes[0].middle()

    def add_adjoint(lines):
        def use(block):
            cols = pl.ds(pl.multiple_of(block * LD, HD), LD)
            high, low = halves(lines[block])
            sh = shi[:, cols]
            acc[...] += dot(sh, high, ((1,), (0,))) + (dot(slo[:, cols], high, ((1,), (0,))) + dot(sh, low, ((1,), (0,))))

        return use

    def flow_part(block, high, low):
        cols = pl.ds(pl.multiple_of(block * LD, HD), LD)
        sh = shi[:, cols]
        return dot(sh, high, ((0,), (0,))) + (dot(slo[:, cols], high, ((0,), (0,))) + dot(sh, low, ((0,), (0,))))

    def primal(balance, later):
        adjoint = acc[0:NB, :]
        at_storage = dot(hot[...], acc[...], ((0,), (0,)), HIGHEST)[0:NB]
        generation, charging = gen[...], chg[...]
        charge_new = jnp.clip(charging - step * (later - at_storage - balance), -clim, clim)
        pad_c[0:NB, :] = 2.0 * charge_new - charging
        output_new = jnp.clip(generation - 0.25 * (cost[...] + adjoint + balance), 0.0, olim)
        gen[...] = output_new
        chg[...] = charge_new
        return 2.0 * output_new - generation - demand[...]

    def flows_begin(output_bar, part, recv, send_sem, recv_sem):
        pad_i[0:NB, :] = output_bar - dot(hot[...], pad_c[...], ((1,), (0,)), HIGHEST)[0:NB]
        injection = pad_i[...]
        high, low = halves(injection)
        total = jnp.broadcast_to(jnp.sum(injection, axis=0, keepdims=True), (ROW, HD))
        for j, (dx, dz) in enumerate(PEERS):
            part[j, 0:LD, :] = flow_part(place.block(dx, dz), high, low)
            part[j, LD : LD + ROW, :] = total
            sends.start(part.at[j], recv.at[j], send_sem.at[j], recv_sem.at[j], place.bus_peer(dx, dz))
        part[7, 0:LD, :] = flow_part(place.bus, high, low)
        part[7, LD : LD + ROW, :] = total

    def flows_end(part, recv, send_sem, recv_sem):
        for j, (dx, dz) in enumerate(PEERS):
            arrived(recv.at[j], send_sem.at[j], recv_sem.at[j], place.bus_peer(dx, dz))
        whole = part[7]
        for j in range(7):
            whole = whole + recv[j]
        return whole[0:LD], whole[LD : LD + 1]

    def line_step(line, flows):
        raised = 4.0 * line + flows
        return 0.25 * (raised - jnp.clip(raised, -llim, llim))

    def level_step(carried):
        level = lstart + carried + dot(pad_c[...], until, ((1,), (0,)), HIGHEST)[0:NB]
        raised = 4.0 * pad_l[0:NB, :] + level
        pad_l[0:NB, :] = 0.25 * (raised - jnp.clip(raised, 0.0, llev))
        return level

    def later_of(carried):
        return carried + dot(pad_l[...], since, ((1,), (0,)), HIGHEST)[0:NB]

    gather1.run(add_adjoint(lines1))
    balance = bal[0:1, :]
    output_bar = primal(balance, later_of(prefixes[0].end(True)))
    prefixes[1].begin(pad_c[...])
    flows_begin(output_bar, part1, recv1, s1s, s1r)
    prefixes[1].middle()
    level_step(prefixes[1].end(False))
    prefixes[2].begin(pad_l[...])
    flows, total = flows_end(part1, recv1, s1s, s1r)
    lines2[place.bus] = line_step(lines1[place.bus], flows)
    gather2 = Gather(place, sends, lines2, LD, 256, g2s, g2r)
    gather2.begin()
    balance = balance + total * (1.0 / float(B + S))
    prefixes[2].middle()

    acc[...] = jnp.zeros((NP, HD), F32)
    gather2.run(add_adjoint(lines2))
    output_bar = primal(balance, later_of(prefixes[2].end(True)))
    prefixes[3].begin(pad_c[...])
    flows_begin(output_bar, part2, recv2, s2s, s2r)
    outs = [pltpu.make_async_copy(gen, gen_o, out_sem.at[0]), pltpu.make_async_copy(chg, chg_o, out_sem.at[1])]
    for copy in outs:
        copy.start()
    prefixes[3].middle()
    level_v[...] = level_step(prefixes[3].end(False))
    ldual[...] = pad_l[0:NB, :]
    more = [pltpu.make_async_copy(level_v, level_o, out_sem.at[2]), pltpu.make_async_copy(ldual, ldual_o, out_sem.at[3])]
    for copy in more:
        copy.start()
    flows, total = flows_end(part2, recv2, s2s, s2r)
    line_v[...] = line_step(lines2[place.bus], flows)
    bal[0:1, :] = balance + total * (1.0 / float(B + S))
    last = [pltpu.make_async_copy(line_v, line_o, out_sem.at[4]), pltpu.make_async_copy(bal, bal_o, out_sem.at[5])]
    for copy in last:
        copy.start()
    for copy in outs + more + last:
        copy.wait()
    sends.finish()


def body(
    line_sensitivity,
    demand,
    unit_cost,
    output_limit,
    output_start,
    line_limit,
    line_dual,
    storage_bus,
    charge_limit,
    charge_start,
    level_start,
    level_limit,
    level_dual,
    balance_dual,
):
    anywhere = pl.BlockSpec(memory_space=pl.ANY)
    block = jax.ShapeDtypeStruct((NB, HD), F32)
    vm = pltpu.VMEM
    dma = pltpu.SemaphoreType.DMA
    scratch = [
        vm((NB, NL), F32),
        vm((NB, HD), F32),
        vm((NB, HD), F32),
        vm((1, NB), F32),
        vm((NB, HD), F32),
        vm((1, NL), F32),
        vm((1, NB), jnp.int32),
        vm((1, NB), F32),
        vm((NB, HD), F32),
        vm((1, NB), F32),
        vm((1, NB), F32),
        vm((NB, HD), F32),
        vm((1, HD), F32),
        vm((LD, HD), F32),
        vm((NP, NL), BF16),
        vm((NP, NL), BF16),
        vm((16, NL), F32),
        vm((8, LD, HD), F32),
        vm((8, LD, HD), F32),
        vm((8, LD + ROW, HD), F32),
        vm((8, LD + ROW, HD), F32),
        vm((7, LD + ROW, HD), F32),
        vm((7, LD + ROW, HD), F32),
        vm((NP, HD), F32),
        vm((NP, HD), F32),
        vm((NP, HD), F32),
        vm((NP, HD), F32),
        vm((NP, NP), F32),
        vm((NB, HD), F32),
        vm((LD, HD), F32),
        vm((4, 2 * GROUP, ROW, NP), F32),
        dma((ARRAYS,)),
        dma((6,)),
        dma((16,)),
        dma((16,)),
        dma((16,)),
        dma((16,)),
        dma((7,)),
        dma((7,)),
        dma((7,)),
        dma((7,)),
        dma((4, 14)),
        dma((4, 14)),
    ]
    generation, charging, level, line, dual, balance = pl.pallas_call(
        kernel,
        out_shape=(block, block, block, jax.ShapeDtypeStruct((LD, HD), F32), block, jax.ShapeDtypeStruct((1, HD), F32)),
        in_specs=[anywhere] * ARRAYS,
        out_specs=[anywhere] * 6,
        scratch_shapes=scratch,
        compiler_params=pltpu.CompilerParams(collective_id=0, has_side_effects=True, vmem_limit_bytes=56 * 1024 * 1024),
    )(
        line_sensitivity,
        demand,
        unit_cost,
        output_limit.reshape(1, NB),
        output_start,
        line_limit.reshape(1, NL),
        line_dual,
        storage_bus.reshape(1, NB),
        charge_limit.reshape(1, NB),
        charge_start,
        level_start.reshape(1, NB),
        level_limit.reshape(1, NB),
        level_dual,
        balance_dual.reshape(1, HD),
    )
    return generation, charging, level, line, dual, balance.reshape(HD)


def solution(mesh):
    both = P("bus", "hour")
    return jax.shard_map(
        body,
        mesh=mesh,
        in_specs=(
            P("bus", None),
            both,
            both,
            P("bus"),
            both,
            P(),
            both,
            P("bus"),
            P("bus"),
            both,
            P("bus"),
            P("bus"),
            both,
            P("hour"),
        ),
        out_specs=(both, both, both, both, both, P("hour")),
        check_vma=False,
    )
```

```python
import jax
import jax.numpy as jnp
from jax import lax
from jax.experimental import pallas as pl
from jax.experimental.pallas import tpu as pltpu
from jax.sharding import PartitionSpec as P

B = 2000
S = 2000
ITERS = 2
HOURS = 8192
NB = 250
NP = 256
HD = 128
LD = 384
NL = 3072
NX = 4
NY = 8
NZ = 4
ROW = 8
MESH = pl.DeviceIdType.MESH
HIGHEST = lax.Precision.HIGHEST
F32 = jnp.float32
BF16 = jnp.bfloat16
PEERS = ((2, 1), (1, 1), (3, 1), (2, 0), (1, 0), (3, 0), (0, 1))
PIECE = 32
ARRAYS = 14


def dot(a, b, dims, precision=None):
    return lax.dot_general(a, b, (dims, ((), ())), precision=precision, preferred_element_type=F32)


def halves(value):
    high = value.astype(BF16)
    return high, (value - high.astype(F32)).astype(BF16)


class Place:
    def __init__(self):
        self.hour = lax.axis_index("hour")
        self.bus = lax.axis_index("bus")
        self.x = self.bus // 2
        self.z = lax.rem(self.bus, 2)
        self.high, self.y, self.core = self.hour // 16, lax.rem(self.hour // 2, NY), lax.rem(self.hour, 2)

    def block(self, dx, dz):
        return lax.rem(self.x + dx + NX, NX) * 2 + lax.rem(self.z + dz, 2)

    def bus_peer(self, dx, dz):
        return (self.hour, self.block(dx, dz))

    def y_peer(self, d):
        return (self.high * 16 + lax.rem(self.y + d + NY, NY) * 2 + self.core, self.bus)

    def z_peer(self, d):
        return (lax.rem(self.high + d, NZ) * 16 + self.y * 2 + self.core, self.bus)

    def core_peer(self):
        return (self.hour + 1 - 2 * self.core, self.bus)


class Sends:
    def __init__(self):
        self.all = []

    def start(self, src, dst, send_sem, recv_sem, device):
        copy = pltpu.make_async_remote_copy(
            src_ref=src, dst_ref=dst, send_sem=send_sem, recv_sem=recv_sem, device_id=device, device_id_type=MESH
        )
        copy.start()
        self.all.append(copy)

    def finish(self):
        for copy in self.all:
            copy.wait_send()


def arrived(ref, send_sem, recv_sem, device):
    pltpu.make_async_remote_copy(
        src_ref=ref, dst_ref=ref, send_sem=send_sem, recv_sem=recv_sem, device_id=device, device_id_type=MESH
    ).wait_recv()


class Gather:
    def __init__(self, place, sends, buf, rows, cut, send_sem, recv_sem):
        h = rows // 2
        self.place, self.sends, self.buf = place, sends, buf
        self.send_sem, self.recv_sem = send_sem, recv_sem
        right, left, across = (1, 0), (3, 0), (0, 1)
        self.plan = {
            "r1": (right, (0, 0), 0, h),
            "r2": (right, (0, 0), h, rows),
            "r3": (right, (3, 0), 0, h),
            "r4": (right, (0, 1), cut, rows),
            "r5": (right, (3, 1), 0, h),
            "l1": (left, (0, 0), h, rows),
            "l2": (left, (0, 0), 0, h),
            "l3": (left, (1, 0), h, rows),
            "l4": (left, (0, 1), 0, rows - cut),
            "l5": (left, (1, 1), h, rows),
            "z1": (across, (0, 0), 0, h),
            "z2": (across, (0, 0), h, rows),
            "z3": (across, (3, 0), 0, h),
            "z4": (across, (1, 0), h, rows),
            "z5": (across, (3, 0), h, cut),
            "z6": (across, (1, 0), rows - cut, h),
        }
        self.number = {key: i for i, key in enumerate(self.plan)}

    def send(self, *keys):
        for key in keys:
            to, block, first, last = self.plan[key]
            ref = self.buf.at[self.place.block(*block), pl.ds(first, last - first)]
            i = self.number[key]
            self.sends.start(ref, ref, self.send_sem.at[i], self.recv_sem.at[i], self.place.bus_peer(*to))

    def wait(self, *keys):
        for key in keys:
            to, block, first, last = self.plan[key]
            at = self.place.block((block[0] - to[0]) % NX, (block[1] + to[1]) % 2)
            ref = self.buf.at[at, pl.ds(first, last - first)]
            i = self.number[key]
            arrived(ref, self.send_sem.at[i], self.recv_sem.at[i], self.place.bus_peer(*to))

    def begin(self):
        self.send("r1", "l1", "z1", "r2", "l2", "z2")

    def run(self, use, beside):
        block = self.place.block
        self.wait("r1")
        self.send("r3", "z3")
        self.wait("l1")
        self.send("l3", "z4")
        beside(1)
        self.wait("r2")
        self.send("z5")
        self.wait("l2")
        self.send("z6")
        self.wait("z1")
        self.send("l4")
        self.wait("z2")
        self.send("r4")
        beside(2)
        use(block(0, 0))
        use(block(3, 0))
        self.wait("z3")
        self.send("r5")
        self.wait("z4")
        self.send("l5")
        beside(3)
        use(block(1, 0))
        use(block(0, 1))
        self.wait("r3", "l3")
        beside(4)
        use(block(2, 0))
        self.wait("z5", "r4")
        use(block(3, 1))
        self.wait("z6", "l4")
        use(block(1, 1))
        beside(5)
        self.wait("r5", "l5")
        use(block(2, 1))


class Columns:
    def __init__(self, place, sends, buf, piece, bus_send, bus_recv, ring_send, ring_recv):
        self.place, self.sends, self.buf, self.piece = place, sends, buf, piece
        self.bus_send, self.bus_recv = bus_send, bus_recv
        self.ring_send, self.ring_recv = ring_send, ring_recv

    def eighth(self):
        return lax.rem(self.place.y, 4) * 2 + self.place.core

    def rows(self, dy, part=None, other=False):
        core = 1 - self.place.core if other else self.place.core
        at = (lax.rem(self.place.y + dy + NY, 4) * 2 + core) * PIECE
        if part is None:
            return self.buf.at[pl.ds(1, 7), pl.ds(pl.multiple_of(at, PIECE), PIECE)]
        half = PIECE // 2
        return self.buf.at[pl.ds(1, 7), pl.ds(pl.multiple_of(at + part * half, half), half)]

    def begin(self):
        place = self.place
        at = pl.multiple_of(self.eighth() * PIECE, PIECE)
        for k in range(1, 8):
            to = lax.rem(place.bus + k, 8)
            src = self.piece.at[:, pl.ds(pl.multiple_of(to * LD, HD), LD)]
            dst = self.buf.at[8 - k, pl.ds(at, PIECE)]
            self.sends.start(src, dst, self.bus_send.at[k - 1], self.bus_recv.at[k - 1], (place.hour, to))

    def pass_on(self, i, ref, device):
        self.sends.start(ref, ref, self.ring_send.at[i], self.ring_recv.at[i], device)

    def came(self, i, ref):
        arrived(ref, self.ring_send.at[i], self.ring_recv.at[i], self.place.core_peer())

    def fetched(self):
        place = self.place
        at = pl.multiple_of(self.eighth() * PIECE, PIECE)
        for k in range(1, 8):
            ref = self.buf.at[8 - k, pl.ds(at, PIECE)]
            arrived(ref, self.bus_send.at[k - 1], self.bus_recv.at[k - 1], (place.hour, lax.rem(place.bus + k, 8)))
        up, down = place.y_peer(1), place.y_peer(-1)
        self.pass_on(0, self.rows(0, 0), up)
        self.pass_on(1, self.rows(0, 1), down)
        self.pass_on(2, self.rows(0, 1), up)
        self.pass_on(3, self.rows(0, 0), down)
        self.pass_on(6, self.rows(0), place.core_peer())

    def first_halves(self):
        self.came(0, self.rows(-1, 0))
        self.pass_on(4, self.rows(-1, 0), self.place.y_peer(1))
        self.came(1, self.rows(1, 1))
        self.pass_on(5, self.rows(1, 1), self.place.y_peer(-1))

    def second_halves(self):
        self.came(2, self.rows(-1, 1))
        self.pass_on(7, self.rows(-1), self.place.core_peer())
        self.came(3, self.rows(1, 0))
        self.pass_on(8, self.rows(1), self.place.core_peer())

    def far_halves(self):
        self.came(4, self.rows(2, 0))
        self.came(5, self.rows(2, 1))
        self.pass_on(9, self.rows(2), self.place.core_peer())

    def end(self):
        for i, dy in ((6, 0), (7, -1), (8, 1), (9, 2)):
            self.came(i, self.rows(dy, other=True))


class Prefix:
    SLOTS = 2 + NY + NZ

    def __init__(self, place, sends, buf, send_sem, recv_sem):
        self.place, self.sends, self.buf = place, sends, buf
        self.send_sem, self.recv_sem = send_sem, recv_sem

    def give(self, i, slot, device):
        ref = self.buf.at[slot]
        self.sends.start(ref, ref, self.send_sem.at[i], self.recv_sem.at[i], device)

    def take(self, i, slot):
        arrived(self.buf.at[slot], self.send_sem.at[i], self.recv_sem.at[i], self.place.core_peer())

    def begin(self, value):
        place = self.place
        self.buf[place.core] = dot(jnp.ones((ROW, HD), F32), value, ((1,), (1,)), HIGHEST)
        self.give(0, place.core, place.core_peer())

    def over_y(self):
        place = self.place
        self.take(0, 1 - place.core)
        self.buf[2 + place.y] = self.buf[0] + self.buf[1]
        for d in (4, 3, 5, 2, 6, 1, 7):
            self.give(d, 2 + place.y, place.y_peer(d))

    def over_z(self):
        place = self.place
        for d in range(1, NY):
            self.take(d, 2 + lax.rem(place.y - d + NY, NY))
        total = self.buf[2]
        for i in range(1, NY):
            total = total + self.buf[2 + i]
        self.buf[2 + NY + place.high] = total
        for d in (2, 1, 3):
            self.give(NY - 1 + d, 2 + NY + place.high, place.z_peer(d))

    def end(self, reverse):
        place = self.place
        for d in range(1, NZ):
            self.take(NY - 1 + d, 2 + NY + lax.rem(place.high - d + NZ, NZ))
        count = self.SLOTS * ROW
        row = lax.broadcasted_iota(jnp.int32, (count, HD), 0)
        slot = row // ROW
        in_core, in_y = slot < 2, (slot >= 2) & (slot < 2 + NY)
        at = jnp.where(in_core, slot, jnp.where(in_y, slot - 2, slot - 2 - NY))
        mine = jnp.where(in_core, place.core, jnp.where(in_y, place.y, place.high))
        reached = (at > mine) if reverse else (at < mine)
        reached = reached & (lax.rem(row, ROW) == 0)
        gathered = self.buf[...].reshape(count, NP)
        return dot(gathered, reached.astype(F32), ((0,), (0,)), HIGHEST)[0:NB]


def kernel(*refs):
    (sens_h, demand_h, cost_h, olim_h, gen_h, llim_h, line_h, sbus_h, clim_h, chg_h, lstart_h, llev_h, ldual_h, bal_h) = refs[:14]
    (gen_o, chg_o, level_o, line_o, ldual_o, bal_o) = refs[14:20]
    (sens, demand, cost, olim_r, gen, llim_r, sbus_r, clim_r, chg, lstart_r, llev_r, ldual, bal) = refs[20:33]
    (shi, slo, tail, lines1, lines2, inj1, inj2, cols, chi, clo, piece, acc, pad_l, pad_c, pad_i, hot, level_v, line_v, pre) = refs[33:52]
    (in_sem, out_sem, g1s, g1r, g2s, g2r, i1s, i1r, i2s, i2r, cbs, cbr, crs, crr, ps, pr) = refs[52:]
    place = Place()
    sends = Sends()

    ins = {}
    for i, (src, dst) in enumerate(
        (
            (line_h, lines1.at[place.bus]),
            (ldual_h, ldual),
            (sens_h, sens),
            (llim_h, llim_r),
            (sbus_h, sbus_r),
            (olim_h, olim_r),
            (clim_h, clim_r),
            (lstart_h, lstart_r),
            (llev_h, llev_r),
            (bal_h, bal),
            (demand_h, demand),
            (cost_h, cost),
            (gen_h, gen),
            (chg_h, chg),
        )
    ):
        ins[i] = pltpu.make_async_copy(src, dst, in_sem.at[i])
        ins[i].start()

    barrier = pltpu.get_barrier_semaphore()
    partners = [place.bus_peer(*d) for d in PEERS]
    partners += [place.core_peer()]
    partners += [place.y_peer(d) for d in range(1, NY)]
    partners += [place.z_peer(d) for d in range(1, NZ)]
    for device in partners:
        pl.semaphore_signal(barrier, inc=1, device_id=device, device_id_type=MESH)

    zeros = jnp.zeros((NP - NB, HD), F32)
    for ref in (pad_l, pad_c, pad_i):
        ref[NB:NP, :] = zeros
    acc[...] = jnp.zeros((NP, HD), F32)
    ins[0].wait()
    pl.semaphore_wait(barrier, len(partners))

    gather1 = Gather(place, sends, lines1, LD, 256, g1s, g1r)
    gather1.begin()
    prefixes = [Prefix(place, sends, pre.at[k], ps.at[k], pr.at[k]) for k in range(4)]
    ins[1].wait()
    pad_l[0:NB, :] = ldual[...]
    prefixes[0].begin(pad_l[...])

    ins[2].wait()
    tail[0:26, :] = sens[224:NB, :]
    tail[26:32, :] = jnp.zeros((6, NL), F32)
    columns = Columns(place, sends, cols, piece, cbs, cbr, crs, crr)
    eighth = columns.eighth()

    @pl.when(eighth < 7)
    def _():
        piece[...] = sens[pl.ds(pl.multiple_of(eighth * PIECE, PIECE), PIECE), :]

    @pl.when(eighth == 7)
    def _():
        piece[...] = tail[...]

    columns.begin()
    first_line = pl.multiple_of(place.bus * LD, HD)
    cols[0, 0:224, :] = sens[0:224, pl.ds(first_line, LD)]
    cols[0, 224:NP, :] = tail[:, pl.ds(first_line, LD)]

    @pl.loop(0, 14)
    def _(i):
        rows = pl.ds(pl.multiple_of(i * 16, 16), 16)
        shi[rows, :], slo[rows, :] = halves(sens[rows, :])

    shi[224:NP, :], slo[224:NP, :] = halves(tail[...])

    for i in range(3, ARRAYS):
        ins[i].wait()

    def column(row, count):
        return jnp.broadcast_to(row, (HD, count)).T

    olim = column(olim_r[0:1, :], NB)
    clim = column(clim_r[0:1, :], NB)
    lstart = column(lstart_r[0:1, :], NB)
    llev = column(llev_r[0:1, :], NB)
    llim = column(llim_r[0:1, pl.ds(first_line, LD)], LD)
    at_bus = lax.broadcasted_iota(jnp.int32, (NP, NB), 0)
    local = sbus_r[0:1, :] - place.bus * NB
    hot[...] = jnp.zeros((NP, NP), F32)
    hot[:, 0:NB] = (at_bus == local).astype(F32)
    hour_at = lax.broadcasted_iota(jnp.int32, (HD, HD), 0)
    hour_to = lax.broadcasted_iota(jnp.int32, (HD, HD), 1)
    until = (hour_at <= hour_to).astype(F32)
    since = (hour_at >= hour_to).astype(F32)
    hour_pos = (place.hour * HD + lax.broadcasted_iota(jnp.int32, (1, HD), 1)).astype(F32)
    step = 1.0 / (float(HOURS) - hour_pos + 4.0)
    prefixes[0].over_y()

    def add_adjoint(lines):
        def use(block):
            cols = pl.ds(pl.multiple_of(block * LD, HD), LD)
            high, low = halves(lines[block])
            sh = shi[:, cols]
            acc[...] += dot(sh, high, ((1,), (0,))) + (dot(slo[:, cols], high, ((1,), (0,))) + dot(sh, low, ((1,), (0,))))

        return use

    def primal(balance, later):
        adjoint = acc[0:NB, :]
        at_storage = dot(hot[...], acc[...], ((0,), (0,)), HIGHEST)[0:NB]
        generation, charging = gen[...], chg[...]
        charge_new = jnp.clip(charging - step * (later - at_storage - balance), -clim, clim)
        pad_c[0:NB, :] = 2.0 * charge_new - charging
        output_new = jnp.clip(generation - 0.25 * (cost[...] + adjoint + balance), 0.0, olim)
        gen[...] = output_new
        chg[...] = charge_new
        return 2.0 * output_new - generation - demand[...]

    def inject(output_bar, buf, send_sem, recv_sem):
        pad_i[0:NB, :] = output_bar - dot(hot[...], pad_c[...], ((1,), (0,)), HIGHEST)[0:NB]
        buf[place.bus] = pad_i[...].T
        gather = Gather(place, sends, buf, HD, 88, send_sem, recv_sem)
        gather.begin()
        return gather

    def split_columns():
        for k in range(8):
            chi[k], clo[k] = halves(cols[k])

    def flows_of(gather, buf, beside):
        sums = [jnp.zeros((HD, LD), F32), jnp.zeros((HD, NP), F32)]

        def use(block):
            k = lax.rem(block - place.bus + 8, 8)
            injection = buf[block]
            high, low = halves(injection)
            ch = chi[k]
            sums[0] += dot(high, ch, ((1,), (0,))) + (dot(low, ch, ((1,), (0,))) + dot(high, clo[k], ((1,), (0,))))
            sums[1] += injection

        gather.run(use, beside)
        total = dot(jnp.ones((ROW, NP), F32), sums[1], ((1,), (1,)), HIGHEST)
        return sums[0].T, total[0:1]

    def line_step(line, flows):
        raised = 4.0 * line + flows
        return 0.25 * (raised - jnp.clip(raised, -llim, llim))

    def level_step(carried):
        level = lstart + carried + dot(pad_c[...], until, ((1,), (0,)), HIGHEST)[0:NB]
        raised = 4.0 * pad_l[0:NB, :] + level
        pad_l[0:NB, :] = 0.25 * (raised - jnp.clip(raised, 0.0, llev))
        return level

    def later_of(carried):
        return carried + dot(pad_l[...], since, ((1,), (0,)), HIGHEST)[0:NB]

    def beside(at):
        if at == 2:
            columns.fetched()
        if at == 3:
            prefixes[0].over_z()
        if at == 5:
            columns.first_halves()

    gather1.run(add_adjoint(lines1), beside)
    balance = bal[0:1, :]
    output_bar = primal(balance, later_of(prefixes[0].end(True)))
    prefixes[1].begin(pad_c[...])
    gather = inject(output_bar, inj1, i1s, i1r)
    prefixes[1].over_y()
    columns.second_halves()

    def beside(at):
        if at == 1:
            columns.far_halves()
        if at == 2:
            columns.end()
            split_columns()
        if at == 3:
            prefixes[1].over_z()

    flows, total = flows_of(gather, inj1, beside)
    lines2[place.bus] = line_step(lines1[place.bus], flows)
    gather2 = Gather(place, sends, lines2, LD, 256, g2s, g2r)
    gather2.begin()
    balance = balance + total * (1.0 / float(B + S))
    level_step(prefixes[1].end(False))
    prefixes[2].begin(pad_l[...])
    acc[...] = jnp.zeros((NP, HD), F32)

    def beside(at):
        if at == 1:
            prefixes[2].over_y()
        if at == 3:
            prefixes[2].over_z()

    gather2.run(add_adjoint(lines2), beside)
    output_bar = primal(balance, later_of(prefixes[2].end(True)))
    prefixes[3].begin(pad_c[...])
    gather = inject(output_bar, inj2, i2s, i2r)
    prefixes[3].over_y()
    outs = [pltpu.make_async_copy(gen, gen_o, out_sem.at[0]), pltpu.make_async_copy(chg, chg_o, out_sem.at[1])]
    outs[0].start()
    outs[1].start()
    flows, total = flows_of(gather, inj2, lambda at: prefixes[3].over_z() if at == 3 else None)
    line_v[...] = line_step(lines2[place.bus], flows)
    bal[0:1, :] = balance + total * (1.0 / float(B + S))
    outs.append(pltpu.make_async_copy(line_v, line_o, out_sem.at[2]))
    outs.append(pltpu.make_async_copy(bal, bal_o, out_sem.at[3]))
    outs[2].start()
    outs[3].start()
    level_v[...] = level_step(prefixes[3].end(False))
    ldual[...] = pad_l[0:NB, :]
    outs.append(pltpu.make_async_copy(level_v, level_o, out_sem.at[4]))
    outs.append(pltpu.make_async_copy(ldual, ldual_o, out_sem.at[5]))
    outs[4].start()
    outs[5].start()
    for copy in outs:
        copy.wait()
    sends.finish()


def store(*refs):
    ins = [pltpu.make_async_copy(refs[i], refs[12 + i], refs[18].at[i]) for i in range(6)]
    outs = [pltpu.make_async_copy(refs[12 + i], refs[6 + i], refs[19].at[i]) for i in range(6)]
    for copy in ins:
        copy.start()
    for copy, out in zip(ins, outs):
        copy.wait()
        out.start()
    for out in outs:
        out.wait()


def body(
    line_sensitivity,
    demand,
    unit_cost,
    output_limit,
    output_start,
    line_limit,
    line_dual,
    storage_bus,
    charge_limit,
    charge_start,
    level_start,
    level_limit,
    level_dual,
    balance_dual,
):
    anywhere = pl.BlockSpec(memory_space=pl.ANY)
    block = jax.ShapeDtypeStruct((NB, HD), F32)
    vm = pltpu.VMEM
    dma = pltpu.SemaphoreType.DMA
    scratch = [
        vm((NB, NL), F32),
        vm((NB, HD), F32),
        vm((NB, HD), F32),
        vm((1, NB), F32),
        vm((NB, HD), F32),
        vm((1, NL), F32),
        vm((1, NB), jnp.int32),
        vm((1, NB), F32),
        vm((NB, HD), F32),
        vm((1, NB), F32),
        vm((1, NB), F32),
        vm((NB, HD), F32),
        vm((1, HD), F32),
        vm((NP, NL), BF16),
        vm((NP, NL), BF16),
        vm((PIECE, NL), F32),
        vm((8, LD, HD), F32),
        vm((8, LD, HD), F32),
        vm((8, HD, NP), F32),
        vm((8, HD, NP), F32),
        vm((8, NP, LD), F32),
        vm((8, NP, LD), BF16),
        vm((8, NP, LD), BF16),
        vm((PIECE, NL), F32),
        vm((NP, HD), F32),
        vm((NP, HD), F32),
        vm((NP, HD), F32),
        vm((NP, HD), F32),
        vm((NP, NP), F32),
        vm((NB, HD), F32),
        vm((LD, HD), F32),
        vm((4, Prefix.SLOTS, ROW, NP), F32),
        dma((ARRAYS,)),
        dma((6,)),
        dma((16,)),
        dma((16,)),
        dma((16,)),
        dma((16,)),
        dma((16,)),
        dma((16,)),
        dma((16,)),
        dma((16,)),
        dma((7,)),
        dma((7,)),
        dma((16,)),
        dma((16,)),
        dma((4, NY + NZ - 1)),
        dma((4, NY + NZ - 1)),
    ]
    shapes = (block, block, block, jax.ShapeDtypeStruct((LD, HD), F32), block, jax.ShapeDtypeStruct((1, HD), F32))
    results = pl.pallas_call(
        kernel,
        out_shape=shapes,
        in_specs=[anywhere] * ARRAYS,
        out_specs=[anywhere] * 6,
        scratch_shapes=scratch,
        compiler_params=pltpu.CompilerParams(collective_id=0, has_side_effects=True, vmem_limit_bytes=56 * 1024 * 1024),
    )(
        line_sensitivity,
        demand,
        unit_cost,
        output_limit.reshape(1, NB),
        output_start,
        line_limit.reshape(1, NL),
        line_dual,
        storage_bus.reshape(1, NB),
        charge_limit.reshape(1, NB),
        charge_start,
        level_start.reshape(1, NB),
        level_limit.reshape(1, NB),
        level_dual,
        balance_dual.reshape(1, HD),
    )
    generation, charging, level, line, dual, balance = pl.pallas_call(
        store,
        out_shape=shapes,
        in_specs=[anywhere] * 6,
        out_specs=[anywhere] * 6,
        scratch_shapes=[vm(shape.shape, F32) for shape in shapes] + [dma((6,)), dma((6,))],
        compiler_params=pltpu.CompilerParams(vmem_limit_bytes=56 * 1024 * 1024),
    )(*results)
    return generation, charging, level, line, dual, balance.reshape(HD)


def solution(mesh):
    both = P("bus", "hour")
    return jax.shard_map(
        body,
        mesh=mesh,
        in_specs=(
            P("bus", None),
            both,
            both,
            P("bus"),
            both,
            P(),
            both,
            P("bus"),
            P("bus"),
            both,
            P("bus"),
            P("bus"),
            both,
            P("hour"),
        ),
        out_specs=(both, both, both, both, both, P("hour")),
        check_vma=False,
    )
```

```python
import jax
import jax.numpy as jnp
from jax import lax
from jax.experimental import pallas as pl
from jax.experimental.pallas import tpu as pltpu
from jax.sharding import PartitionSpec as P

B = 2000
S = 2000
ITERS = 2
HOURS = 8192
NB = 250
NP = 256
HD = 128
LD = 384
NL = 3072
NX = 4
NY = 8
NZ = 4
ROW = 8
MESH = pl.DeviceIdType.MESH
HIGHEST = lax.Precision.HIGHEST
F32 = jnp.float32
BF16 = jnp.bfloat16
PEERS = ((2, 1), (1, 1), (3, 1), (2, 0), (1, 0), (3, 0), (0, 1))
PIECE = 32
ARRAYS = 14


def dot(a, b, dims, precision=None):
    return lax.dot_general(a, b, (dims, ((), ())), precision=precision, preferred_element_type=F32)


def halves(value):
    high = value.astype(BF16)
    return high, (value - high.astype(F32)).astype(BF16)


def column(row, count):
    return jnp.broadcast_to(row, (HD, count)).T


def dot_exact(a, b, dims):
    if a.dtype == BF16:
        high, low = halves(b)
        return dot(a, high, dims) + dot(a, low, dims)
    high, low = halves(a)
    return dot(high, b, dims) + dot(low, b, dims)


class Place:
    def __init__(self):
        self.hour = lax.axis_index("hour")
        self.bus = lax.axis_index("bus")
        self.x = self.bus // 2
        self.z = lax.rem(self.bus, 2)
        self.high, self.y, self.core = self.hour // 16, lax.rem(self.hour // 2, NY), lax.rem(self.hour, 2)

    def block(self, dx, dz):
        return lax.rem(self.x + dx + NX, NX) * 2 + lax.rem(self.z + dz, 2)

    def bus_peer(self, dx, dz):
        return (self.hour, self.block(dx, dz))

    def y_peer(self, d):
        return (self.high * 16 + lax.rem(self.y + d + NY, NY) * 2 + self.core, self.bus)

    def z_peer(self, d):
        return (lax.rem(self.high + d, NZ) * 16 + self.y * 2 + self.core, self.bus)

    def core_peer(self):
        return (self.hour + 1 - 2 * self.core, self.bus)


class Sends:
    def __init__(self):
        self.groups = []

    def start(self, src, dst, send_sem, recv_sem, device):
        pltpu.make_async_remote_copy(
            src_ref=src, dst_ref=dst, send_sem=send_sem, recv_sem=recv_sem, device_id=device, device_id_type=MESH
        ).start()

    def group(self, ref, send_sem):
        self.groups.append((ref, send_sem))

    def finish(self):
        for ref, sem in self.groups:
            pltpu.make_async_copy(ref, ref, sem).wait()


def arrived(ref, recv_sem):
    pltpu.make_async_copy(ref, ref, recv_sem).wait()


class Gather:
    def __init__(self, place, sends, buf, rows, cut, send_sem, recv_sem):
        h = rows // 2
        self.place, self.sends, self.buf = place, sends, buf
        self.send_sem, self.recv_sem = send_sem, recv_sem
        right, left, across = (1, 0), (3, 0), (0, 1)
        self.plan = {
            "r1": (right, (0, 0), 0, h),
            "r2": (right, (0, 0), h, rows),
            "r3": (right, (3, 0), 0, h),
            "r4": (right, (0, 1), cut, rows),
            "r5": (right, (3, 1), 0, h),
            "l1": (left, (0, 0), h, rows),
            "l2": (left, (0, 0), 0, h),
            "l3": (left, (1, 0), h, rows),
            "l4": (left, (0, 1), 0, rows - cut),
            "l5": (left, (1, 1), h, rows),
            "z1": (across, (0, 0), 0, h),
            "z2": (across, (0, 0), h, rows),
            "z3": (across, (3, 0), 0, h),
            "z4": (across, (1, 0), h, rows),
            "z5": (across, (3, 0), h, cut),
            "z6": (across, (1, 0), rows - cut, h),
        }
        self.number = {key: i for i, key in enumerate(self.plan)}

    def send(self, *keys):
        for key in keys:
            to, block, first, last = self.plan[key]
            ref = self.buf.at[self.place.block(*block), pl.ds(first, last - first)]
            i = self.number[key]
            self.sends.start(ref, ref, self.send_sem, self.recv_sem.at[i], self.place.bus_peer(*to))

    def wait(self, *keys):
        for key in keys:
            to, block, first, last = self.plan[key]
            at = self.place.block((block[0] - to[0]) % NX, (block[1] + to[1]) % 2)
            ref = self.buf.at[at, pl.ds(first, last - first)]
            i = self.number[key]
            arrived(ref, self.recv_sem.at[i])

    def begin(self):
        self.send("r1", "l1", "z1", "r2", "l2", "z2")
        self.sends.group(self.buf.at[pl.ds(0, 7)], self.send_sem)

    def run(self, use, beside):
        block = self.place.block
        self.wait("r1")
        self.send("r3", "z3")
        self.wait("l1")
        self.send("l3", "z4")
        beside(1)
        self.wait("r2")
        self.send("z5")
        self.wait("l2")
        self.send("z6")
        self.wait("z1")
        self.send("l4")
        self.wait("z2")
        self.send("r4")
        beside(2)
        use(block(0, 0))
        use(block(3, 0))
        self.wait("z3")
        self.send("r5")
        self.wait("z4")
        self.send("l5")
        beside(3)
        use(block(1, 0))
        use(block(0, 1))
        self.wait("r3", "l3")
        beside(4)
        use(block(2, 0))
        self.wait("z5", "r4")
        use(block(3, 1))
        self.wait("z6", "l4")
        use(block(1, 1))
        beside(5)
        self.wait("r5", "l5")
        use(block(2, 1))


class Columns:
    def __init__(self, place, sends, buf, piece, bus_send, bus_recv, ring_send, ring_recv):
        self.place, self.sends, self.buf, self.piece = place, sends, buf, piece
        self.bus_send, self.bus_recv = bus_send, bus_recv
        self.ring_send, self.ring_recv = ring_send, ring_recv

    def eighth(self):
        return lax.rem(self.place.y, 4) * 2 + self.place.core

    def rows(self, dy, part=None, other=False):
        core = 1 - self.place.core if other else self.place.core
        at = (lax.rem(self.place.y + dy + NY, 4) * 2 + core) * PIECE
        if part is None:
            return self.buf.at[pl.ds(1, 7), pl.ds(pl.multiple_of(at, PIECE), PIECE)]
        half = PIECE // 2
        return self.buf.at[pl.ds(1, 7), pl.ds(pl.multiple_of(at + part * half, half), half)]

    def begin(self):
        place = self.place
        at = pl.multiple_of(self.eighth() * PIECE, PIECE)
        for k in range(1, 8):
            to = lax.rem(place.bus + k, 8)
            src = self.piece.at[:, pl.ds(pl.multiple_of(to * LD, HD), LD)]
            dst = self.buf.at[8 - k, pl.ds(at, PIECE)]
            self.sends.start(src, dst, self.bus_send, self.bus_recv, (place.hour, to))

        self.sends.group(self.rows(0), self.bus_send)
        self.sends.group(self.buf.at[pl.ds(1, 7), pl.ds(0, 7 * PIECE)], self.ring_send)

    def pass_on(self, i, ref, device):
        self.sends.start(ref, ref, self.ring_send, self.ring_recv.at[i], device)

    def came(self, i, ref):
        arrived(ref, self.ring_recv.at[i])

    def fetched(self):
        place = self.place
        arrived(self.rows(0), self.bus_recv)
        up, down = place.y_peer(1), place.y_peer(-1)
        self.pass_on(0, self.rows(0, 0), up)
        self.pass_on(1, self.rows(0, 1), down)
        self.pass_on(2, self.rows(0, 1), up)
        self.pass_on(3, self.rows(0, 0), down)
        self.pass_on(6, self.rows(0), place.core_peer())

    def first_halves(self):
        self.came(0, self.rows(-1, 0))
        self.pass_on(4, self.rows(-1, 0), self.place.y_peer(1))
        self.came(1, self.rows(1, 1))
        self.pass_on(5, self.rows(1, 1), self.place.y_peer(-1))

    def second_halves(self):
        self.came(2, self.rows(-1, 1))
        self.pass_on(7, self.rows(-1), self.place.core_peer())
        self.came(3, self.rows(1, 0))
        self.pass_on(8, self.rows(1), self.place.core_peer())

    def far_halves(self):
        self.came(4, self.rows(2, 0))
        self.came(5, self.rows(2, 1))
        self.pass_on(9, self.rows(2), self.place.core_peer())

    def end(self):
        for i, dy in ((6, 0), (7, -1), (8, 1), (9, 2)):
            self.came(i, self.rows(dy, other=True))


class Prefix:
    SLOTS = 2 + NY + NZ

    def __init__(self, place, sends, buf, send_sem, recv_sem):
        self.place, self.sends, self.buf = place, sends, buf
        self.send_sem, self.recv_sem = send_sem, recv_sem

    def give(self, stage, slot, devices):
        ref = self.buf.at[slot]
        for device in devices:
            self.sends.start(ref, ref, self.send_sem.at[stage], self.recv_sem.at[stage], device)
        self.sends.group(self.buf.at[pl.ds(0, len(devices))], self.send_sem.at[stage])

    def take(self, stage, count):
        arrived(self.buf.at[pl.ds(0, count)], self.recv_sem.at[stage])

    def begin(self, value):
        place = self.place
        self.buf[place.core] = dot(jnp.ones((ROW, HD), F32), value, ((1,), (1,)), HIGHEST)[0:1]
        self.give(0, place.core, [place.core_peer()])

    def over_y(self):
        place = self.place
        self.take(0, 1)
        self.buf[2 + place.y] = self.buf[0] + self.buf[1]
        self.give(1, 2 + place.y, [place.y_peer(d) for d in (4, 3, 5, 2, 6, 1, 7)])

    def over_z(self):
        place = self.place
        self.take(1, NY - 1)
        total = self.buf[2]
        for i in range(1, NY):
            total = total + self.buf[2 + i]
        self.buf[2 + NY + place.high] = total
        self.give(2, 2 + NY + place.high, [place.z_peer(d) for d in (2, 1, 3)])

    def end(self, reverse):
        place = self.place
        self.take(2, NZ - 1)
        row = jnp.zeros((1, NP), F32)
        for base, count, mine in ((0, 2, place.core), (2, NY, place.y), (2 + NY, NZ, place.high)):
            for i in range(count):
                reached = (mine < i) if reverse else (mine > i)
                row = row + self.buf[base + i] * jnp.where(reached, 1.0, 0.0)
        return column(row, NP)[0:NB]


def kernel(*refs):
    (sens_h, demand_h, cost_h, olim_h, gen_h, llim_h, line_h, sbus_h, clim_h, chg_h, lstart_h, llev_h, ldual_h, bal_h) = refs[:14]
    (gen_o, chg_o, level_o, line_o, ldual_o, bal_o) = refs[14:20]
    (sens, demand, cost, olim_r, gen, llim_r, sbus_r, clim_r, chg, lstart_r, llev_r, ldual, bal) = refs[20:33]
    (shi, slo, tail, lines1, lines2, inj1, inj2, cols, chi, clo, piece, acc, pad_l, pad_c, pad_i, hot, hot_t, spread, level_v, line_v, pre) = refs[33:54]
    (in_sem, out_sem, g1s, g1r, g2s, g2r, i1s, i1r, i2s, i2r, cbs, cbr, crs, crr, ps, pr) = refs[54:]
    place = Place()
    sends = Sends()

    ins = {}
    for i, (src, dst) in enumerate(
        (
            (line_h, lines1.at[place.bus]),
            (ldual_h, ldual),
            (sens_h, sens),
            (llim_h, llim_r),
            (sbus_h, sbus_r),
            (olim_h, olim_r),
            (clim_h, clim_r),
            (lstart_h, lstart_r),
            (llev_h, llev_r),
            (bal_h, bal),
            (demand_h, demand),
            (cost_h, cost),
            (gen_h, gen),
            (chg_h, chg),
        )
    ):
        ins[i] = pltpu.make_async_copy(src, dst, in_sem.at[i])
        ins[i].start()

    barrier = pltpu.get_barrier_semaphore()
    partners = [place.bus_peer(*d) for d in PEERS]
    partners += [place.core_peer()]
    partners += [place.y_peer(d) for d in range(1, NY)]
    partners += [place.z_peer(d) for d in range(1, NZ)]
    for device in partners:
        pl.semaphore_signal(barrier, inc=1, device_id=device, device_id_type=MESH)

    zeros = jnp.zeros((NP - NB, HD), F32)
    for ref in (pad_l, pad_c, pad_i):
        ref[NB:NP, :] = zeros
    acc[...] = jnp.zeros((NP, HD), F32)
    ins[0].wait()
    pl.semaphore_wait(barrier, len(partners))

    gather1 = Gather(place, sends, lines1, LD, 256, g1s, g1r)
    gather1.begin()
    prefixes = [Prefix(place, sends, pre.at[k], ps.at[k], pr.at[k]) for k in range(4)]
    ins[1].wait()
    pad_l[0:NB, :] = ldual[...]
    prefixes[0].begin(pad_l[...])
    ins[2].wait()
    tail[0:26, :] = sens[224:NB, :]
    tail[26:32, :] = jnp.zeros((6, NL), F32)
    columns = Columns(place, sends, cols, piece, cbs, cbr, crs, crr)
    eighth = columns.eighth()

    @pl.when(eighth < 7)
    def _():
        piece[...] = sens[pl.ds(pl.multiple_of(eighth * PIECE, PIECE), PIECE), :]

    @pl.when(eighth == 7)
    def _():
        piece[...] = tail[...]

    columns.begin()
    prefixes[0].over_y()
    first_line = pl.multiple_of(place.bus * LD, HD)
    cols[0, 0:224, :] = sens[0:224, pl.ds(first_line, LD)]
    cols[0, 224:NP, :] = tail[:, pl.ds(first_line, LD)]

    @pl.loop(0, 14)
    def _(i):
        rows = pl.ds(pl.multiple_of(i * 16, 16), 16)
        shi[rows, :], slo[rows, :] = halves(sens[rows, :])

    shi[224:NP, :], slo[224:NP, :] = halves(tail[...])

    for i in range(3, ARRAYS):
        ins[i].wait()

    olim = column(olim_r[0:1, :], NB)
    clim = column(clim_r[0:1, :], NB)
    lstart = column(lstart_r[0:1, :], NB)
    llev = column(llev_r[0:1, :], NB)
    llim = column(llim_r[0:1, pl.ds(first_line, LD)], LD)
    at_bus = lax.broadcasted_iota(jnp.int32, (NP, NB), 0)
    local = sbus_r[0:1, :] - place.bus * NB
    spread[...] = jnp.zeros((NP, NP), F32)
    spread[:, 0:NB] = (at_bus == local).astype(F32)
    hot[...] = spread[...].astype(BF16)
    hot_t[...] = spread[...].T.astype(BF16)
    hour_at = lax.broadcasted_iota(jnp.int32, (HD, HD), 0)
    hour_to = lax.broadcasted_iota(jnp.int32, (HD, HD), 1)
    until = (hour_at <= hour_to).astype(F32).astype(BF16)
    since = (hour_at >= hour_to).astype(F32).astype(BF16)
    hour_pos = (place.hour * HD + lax.broadcasted_iota(jnp.int32, (1, HD), 1)).astype(F32)
    step = 1.0 / (float(HOURS) - hour_pos + 4.0)

    def add_adjoint(lines):
        def use(block):
            cols = pl.ds(pl.multiple_of(block * LD, HD), LD)
            high, low = halves(lines[block])
            sh = shi[:, cols]
            acc[...] += dot(sh, high, ((1,), (0,))) + (dot(slo[:, cols], high, ((1,), (0,))) + dot(sh, low, ((1,), (0,))))

        return use

    def primal(balance, later, prefix):
        adjoint = acc[0:NB, :]
        at_storage = dot_exact(hot_t[...], acc[...], ((1,), (0,)))[0:NB]
        generation, charging = gen[...], chg[...]
        charge_new = jnp.clip(charging - step * (later - at_storage - balance), -clim, clim)
        pad_c[0:NB, :] = 2.0 * charge_new - charging
        prefix.begin(pad_c[...])
        output_new = jnp.clip(generation - 0.25 * (cost[...] + adjoint + balance), 0.0, olim)
        gen[...] = output_new
        chg[...] = charge_new
        return 2.0 * output_new - generation - demand[...]

    def inject(output_bar, buf, send_sem, recv_sem, prefix):
        pad_i[0:NB, :] = output_bar - dot_exact(hot[...], pad_c[...], ((1,), (0,)))[0:NB]
        prefix.over_y()
        buf[place.bus] = pad_i[...].T
        gather = Gather(place, sends, buf, HD, 88, send_sem, recv_sem)
        gather.begin()
        return gather

    def split_columns():
        for k in range(8):
            chi[k], clo[k] = halves(cols[k])

    def flows_of(gather, buf, beside):
        sums = [jnp.zeros((HD, LD), F32), jnp.zeros((HD, NP), F32)]

        def use(block):
            k = lax.rem(block - place.bus + 8, 8)
            injection = buf[block]
            high, low = halves(injection)
            ch = chi[k]
            sums[0] += dot(high, ch, ((1,), (0,))) + (dot(low, ch, ((1,), (0,))) + dot(high, clo[k], ((1,), (0,))))
            sums[1] += injection

        gather.run(use, beside)
        total = dot(jnp.ones((ROW, NP), F32), sums[1], ((1,), (1,)), HIGHEST)
        return sums[0].T, total[0:1]

    def line_step(line, flows):
        raised = 4.0 * line + flows
        return 0.25 * (raised - jnp.clip(raised, -llim, llim))

    def level_step(carried):
        level = lstart + carried + dot_exact(pad_c[...], until, ((1,), (0,)))[0:NB]
        raised = 4.0 * pad_l[0:NB, :] + level
        pad_l[0:NB, :] = 0.25 * (raised - jnp.clip(raised, 0.0, llev))
        return level

    def later_of(carried):
        return carried + dot_exact(pad_l[...], since, ((1,), (0,)))[0:NB]

    def beside(at):
        if at == 2:
            prefixes[0].over_z()
            columns.fetched()
        if at == 5:
            columns.first_halves()

    gather1.run(add_adjoint(lines1), beside)
    balance = bal[0:1, :]
    output_bar = primal(balance, later_of(prefixes[0].end(True)), prefixes[1])
    gather = inject(output_bar, inj1, i1s, i1r, prefixes[1])
    columns.second_halves()

    def beside(at):
        if at == 1:
            columns.far_halves()
        if at == 2:
            prefixes[1].over_z()
            columns.end()
            split_columns()

    flows, total = flows_of(gather, inj1, beside)
    lines2[place.bus] = line_step(lines1[place.bus], flows)
    gather2 = Gather(place, sends, lines2, LD, 256, g2s, g2r)
    gather2.begin()
    balance = balance + total * (1.0 / float(B + S))
    level_step(prefixes[1].end(False))
    prefixes[2].begin(pad_l[...])
    acc[...] = jnp.zeros((NP, HD), F32)
    prefixes[2].over_y()

    def beside(at):
        if at == 3:
            prefixes[2].over_z()

    gather2.run(add_adjoint(lines2), beside)
    output_bar = primal(balance, later_of(prefixes[2].end(True)), prefixes[3])
    gather = inject(output_bar, inj2, i2s, i2r, prefixes[3])
    outs = [pltpu.make_async_copy(gen, gen_o, out_sem.at[0]), pltpu.make_async_copy(chg, chg_o, out_sem.at[1])]
    outs[0].start()
    outs[1].start()
    flows, total = flows_of(gather, inj2, lambda at: prefixes[3].over_z() if at == 2 else None)
    line_v[...] = line_step(lines2[place.bus], flows)
    bal[0:1, :] = balance + total * (1.0 / float(B + S))
    outs.append(pltpu.make_async_copy(line_v, line_o, out_sem.at[2]))
    outs.append(pltpu.make_async_copy(bal, bal_o, out_sem.at[3]))
    outs[2].start()
    outs[3].start()
    level_v[...] = level_step(prefixes[3].end(False))
    ldual[...] = pad_l[0:NB, :]
    outs.append(pltpu.make_async_copy(level_v, level_o, out_sem.at[4]))
    outs.append(pltpu.make_async_copy(ldual, ldual_o, out_sem.at[5]))
    outs[4].start()
    outs[5].start()
    for copy in outs:
        copy.wait()
    sends.finish()


def store(*refs):
    copies = [pltpu.make_async_copy(refs[i], refs[6 + i], refs[12].at[i]) for i in range(6)]
    for copy in copies:
        copy.start()
    for copy in copies:
        copy.wait()


def body(
    line_sensitivity,
    demand,
    unit_cost,
    output_limit,
    output_start,
    line_limit,
    line_dual,
    storage_bus,
    charge_limit,
    charge_start,
    level_start,
    level_limit,
    level_dual,
    balance_dual,
):
    anywhere = pl.BlockSpec(memory_space=pl.ANY)
    block = jax.ShapeDtypeStruct((NB, HD), F32)
    vm = pltpu.VMEM
    dma = pltpu.SemaphoreType.DMA
    scratch = [
        vm((NB, NL), F32),
        vm((NB, HD), F32),
        vm((NB, HD), F32),
        vm((1, NB), F32),
        vm((NB, HD), F32),
        vm((1, NL), F32),
        vm((1, NB), jnp.int32),
        vm((1, NB), F32),
        vm((NB, HD), F32),
        vm((1, NB), F32),
        vm((1, NB), F32),
        vm((NB, HD), F32),
        vm((1, HD), F32),
        vm((NP, NL), BF16),
        vm((NP, NL), BF16),
        vm((PIECE, NL), F32),
        vm((8, LD, HD), F32),
        vm((8, LD, HD), F32),
        vm((8, HD, NP), F32),
        vm((8, HD, NP), F32),
        vm((8, NP, LD), F32),
        vm((8, NP, LD), BF16),
        vm((8, NP, LD), BF16),
        vm((PIECE, NL), F32),
        vm((NP, HD), F32),
        vm((NP, HD), F32),
        vm((NP, HD), F32),
        vm((NP, HD), F32),
        vm((NP, NP), BF16),
        vm((NP, NP), BF16),
        vm((NP, NP), F32),
        vm((NB, HD), F32),
        vm((LD, HD), F32),
        vm((4, Prefix.SLOTS, 1, NP), F32),
        dma((ARRAYS,)),
        dma((6,)),
        dma,
        dma((16,)),
        dma,
        dma((16,)),
        dma,
        dma((16,)),
        dma,
        dma((16,)),
        dma,
        dma,
        dma,
        dma((10,)),
        dma((4, 3)),
        dma((4, 3)),
    ]
    shapes = (block, block, block, jax.ShapeDtypeStruct((LD, HD), F32), block, jax.ShapeDtypeStruct((1, HD), F32))
    results = pl.pallas_call(
        kernel,
        out_shape=tuple(pltpu.VMEM(shape.shape, F32) for shape in shapes),
        in_specs=[anywhere] * ARRAYS,
        out_specs=[anywhere] * 6,
        scratch_shapes=scratch,
        compiler_params=pltpu.CompilerParams(collective_id=0, has_side_effects=True, vmem_limit_bytes=56 * 1024 * 1024),
    )(
        line_sensitivity,
        demand,
        unit_cost,
        output_limit.reshape(1, NB),
        output_start,
        line_limit.reshape(1, NL),
        line_dual,
        storage_bus.reshape(1, NB),
        charge_limit.reshape(1, NB),
        charge_start,
        level_start.reshape(1, NB),
        level_limit.reshape(1, NB),
        level_dual,
        balance_dual.reshape(1, HD),
    )
    generation, charging, level, line, dual, balance = pl.pallas_call(
        store,
        out_shape=shapes,
        in_specs=[anywhere] * 6,
        out_specs=[anywhere] * 6,
        scratch_shapes=[dma((6,))],
        compiler_params=pltpu.CompilerParams(vmem_limit_bytes=32 * 1024 * 1024),
    )(*[pltpu.with_memory_space_constraint(result, pltpu.VMEM) for result in results])
    return generation, charging, level, line, dual, balance.reshape(HD)


def solution(mesh):
    both = P("bus", "hour")
    return jax.shard_map(
        body,
        mesh=mesh,
        in_specs=(
            P("bus", None),
            both,
            both,
            P("bus"),
            both,
            P(),
            both,
            P("bus"),
            P("bus"),
            both,
            P("bus"),
            P("bus"),
            both,
            P("hour"),
        ),
        out_specs=(both, both, both, both, both, P("hour")),
        check_vma=False,
    )
```

```python
import jax
import jax.numpy as jnp
from jax import lax
from jax.experimental import pallas as pl
from jax.experimental.pallas import tpu as pltpu
from jax.sharding import PartitionSpec as P

B = 2000
S = 2000
ITERS = 2
HOURS = 8192
NB = 250
NP = 256
HD = 128
LD = 384
NL = 3072
NX = 4
NY = 8
NZ = 4
ROW = 8
MESH = pl.DeviceIdType.MESH
HIGHEST = lax.Precision.HIGHEST
F32 = jnp.float32
BF16 = jnp.bfloat16
PEERS = ((2, 1), (1, 1), (3, 1), (2, 0), (1, 0), (3, 0), (0, 1))
PIECE = 32
ARRAYS = 14


def dot(a, b, dims, precision=None):
    return lax.dot_general(a, b, (dims, ((), ())), precision=precision, preferred_element_type=F32)


def halves(value):
    high = value.astype(BF16)
    return high, (value - high.astype(F32)).astype(BF16)


def column(row, count):
    return jnp.broadcast_to(row, (HD, count)).T


def dot_exact(a, b, dims):
    if a.dtype == BF16:
        high, low = halves(b)
        return dot(a, high, dims) + dot(a, low, dims)
    high, low = halves(a)
    return dot(high, b, dims) + dot(low, b, dims)


class Place:
    def __init__(self):
        self.hour = lax.axis_index("hour")
        self.bus = lax.axis_index("bus")
        self.x = self.bus // 2
        self.z = lax.rem(self.bus, 2)
        self.high, self.y, self.core = self.hour // 16, lax.rem(self.hour // 2, NY), lax.rem(self.hour, 2)

    def block(self, dx, dz):
        return lax.rem(self.x + dx + NX, NX) * 2 + lax.rem(self.z + dz, 2)

    def bus_peer(self, dx, dz):
        return (self.hour, self.block(dx, dz))

    def y_peer(self, d):
        return (self.high * 16 + lax.rem(self.y + d + NY, NY) * 2 + self.core, self.bus)

    def z_peer(self, d):
        return (lax.rem(self.high + d, NZ) * 16 + self.y * 2 + self.core, self.bus)

    def core_peer(self):
        return (self.hour + 1 - 2 * self.core, self.bus)


class Sends:
    def __init__(self):
        self.groups = []

    def start(self, src, dst, send_sem, recv_sem, device):
        pltpu.make_async_remote_copy(
            src_ref=src, dst_ref=dst, send_sem=send_sem, recv_sem=recv_sem, device_id=device, device_id_type=MESH
        ).start()

    def group(self, ref, send_sem):
        self.groups.append((ref, send_sem))

    def finish(self):
        for ref, sem in self.groups:
            pltpu.make_async_copy(ref, ref, sem).wait()


def arrived(ref, recv_sem):
    pltpu.make_async_copy(ref, ref, recv_sem).wait()


class Gather:
    def __init__(self, place, sends, buf, rows, cut, send_sem, recv_sem):
        h = rows // 2
        self.place, self.sends, self.buf = place, sends, buf
        self.send_sem, self.recv_sem = send_sem, recv_sem
        right, left, across = (1, 0), (3, 0), (0, 1)
        self.plan = {
            "r1": (right, (0, 0), 0, h),
            "r2": (right, (0, 0), h, rows),
            "r3": (right, (3, 0), 0, h),
            "r4": (right, (0, 1), cut, rows),
            "r5": (right, (3, 1), 0, h),
            "l1": (left, (0, 0), h, rows),
            "l2": (left, (0, 0), 0, h),
            "l3": (left, (1, 0), h, rows),
            "l4": (left, (0, 1), 0, rows - cut),
            "l5": (left, (1, 1), h, rows),
            "z1": (across, (0, 0), 0, h),
            "z2": (across, (0, 0), h, rows),
            "z3": (across, (3, 0), 0, h),
            "z4": (across, (1, 0), h, rows),
            "z5": (across, (3, 0), h, cut),
            "z6": (across, (1, 0), rows - cut, h),
        }
        self.number = {key: i for i, key in enumerate(self.plan)}

    def send(self, *keys):
        for key in keys:
            to, block, first, last = self.plan[key]
            ref = self.buf.at[self.place.block(*block), pl.ds(first, last - first)]
            i = self.number[key]
            self.sends.start(ref, ref, self.send_sem, self.recv_sem.at[i], self.place.bus_peer(*to))

    def wait(self, *keys):
        for key in keys:
            to, block, first, last = self.plan[key]
            at = self.place.block((block[0] - to[0]) % NX, (block[1] + to[1]) % 2)
            ref = self.buf.at[at, pl.ds(first, last - first)]
            i = self.number[key]
            arrived(ref, self.recv_sem.at[i])

    def begin(self):
        self.send("r1", "l1", "z1", "r2", "l2", "z2")
        self.sends.group(self.buf.at[pl.ds(0, 7)], self.send_sem)

    def run(self, use, beside):
        block = self.place.block
        self.wait("r1")
        self.send("r3", "z3")
        self.wait("l1")
        self.send("l3", "z4")
        beside(1)
        self.wait("r2")
        self.send("z5")
        self.wait("l2")
        self.send("z6")
        self.wait("z1")
        self.send("l4")
        self.wait("z2")
        self.send("r4")
        beside(2)
        use(block(0, 0))
        use(block(3, 0))
        self.wait("z3")
        self.send("r5")
        self.wait("z4")
        self.send("l5")
        beside(3)
        use(block(1, 0))
        use(block(0, 1))
        self.wait("r3", "l3")
        beside(4)
        use(block(2, 0))
        self.wait("z5", "r4")
        use(block(3, 1))
        self.wait("z6", "l4")
        use(block(1, 1))
        beside(5)
        self.wait("r5", "l5")
        use(block(2, 1))


class Columns:
    def __init__(self, place, sends, buf, piece, bus_send, bus_recv, ring_send, ring_recv):
        self.place, self.sends, self.buf, self.piece = place, sends, buf, piece
        self.bus_send, self.bus_recv = bus_send, bus_recv
        self.ring_send, self.ring_recv = ring_send, ring_recv

    def eighth(self):
        return lax.rem(self.place.y, 4) * 2 + self.place.core

    def rows(self, dy, part=None, other=False):
        core = 1 - self.place.core if other else self.place.core
        at = (lax.rem(self.place.y + dy + NY, 4) * 2 + core) * PIECE
        if part is None:
            return self.buf.at[pl.ds(1, 7), pl.ds(pl.multiple_of(at, PIECE), PIECE)]
        half = PIECE // 2
        return self.buf.at[pl.ds(1, 7), pl.ds(pl.multiple_of(at + part * half, half), half)]

    def begin(self):
        place = self.place
        at = pl.multiple_of(self.eighth() * PIECE, PIECE)
        for k in range(1, 8):
            to = lax.rem(place.bus + k, 8)
            src = self.piece.at[:, pl.ds(pl.multiple_of(to * LD, HD), LD)]
            dst = self.buf.at[8 - k, pl.ds(at, PIECE)]
            self.sends.start(src, dst, self.bus_send, self.bus_recv, (place.hour, to))

        self.sends.group(self.rows(0), self.bus_send)
        self.sends.group(self.buf.at[pl.ds(1, 7), pl.ds(0, 7 * PIECE)], self.ring_send)

    def pass_on(self, i, ref, device):
        self.sends.start(ref, ref, self.ring_send, self.ring_recv.at[i], device)

    def came(self, i, ref):
        arrived(ref, self.ring_recv.at[i])

    def fetched(self):
        place = self.place
        arrived(self.rows(0), self.bus_recv)
        up, down = place.y_peer(1), place.y_peer(-1)
        self.pass_on(0, self.rows(0, 0), up)
        self.pass_on(1, self.rows(0, 1), down)
        self.pass_on(2, self.rows(0, 1), up)
        self.pass_on(3, self.rows(0, 0), down)
        self.pass_on(6, self.rows(0), place.core_peer())

    def first_halves(self):
        self.came(0, self.rows(-1, 0))
        self.pass_on(4, self.rows(-1, 0), self.place.y_peer(1))
        self.came(1, self.rows(1, 1))
        self.pass_on(5, self.rows(1, 1), self.place.y_peer(-1))

    def second_halves(self):
        self.came(2, self.rows(-1, 1))
        self.pass_on(7, self.rows(-1), self.place.core_peer())
        self.came(3, self.rows(1, 0))
        self.pass_on(8, self.rows(1), self.place.core_peer())

    def far_halves(self):
        self.came(4, self.rows(2, 0))
        self.came(5, self.rows(2, 1))
        self.pass_on(9, self.rows(2), self.place.core_peer())

    def end(self):
        for i, dy in ((6, 0), (7, -1), (8, 1), (9, 2)):
            self.came(i, self.rows(dy, other=True))


class Prefix:
    SLOTS = 2 + NY + NZ

    def __init__(self, place, sends, buf, send_sem, recv_sem):
        self.place, self.sends, self.buf = place, sends, buf
        self.send_sem, self.recv_sem = send_sem, recv_sem

    def give(self, stage, slot, devices):
        ref = self.buf.at[slot]
        for device in devices:
            self.sends.start(ref, ref, self.send_sem.at[stage], self.recv_sem.at[stage], device)
        self.sends.group(self.buf.at[pl.ds(0, len(devices))], self.send_sem.at[stage])

    def take(self, stage, count):
        arrived(self.buf.at[pl.ds(0, count)], self.recv_sem.at[stage])

    def begin(self, value):
        place = self.place
        self.buf[place.core] = dot(jnp.ones((ROW, HD), F32), value, ((1,), (1,)), HIGHEST)[0:1]
        self.give(0, place.core, [place.core_peer()])

    def over_y(self):
        place = self.place
        self.take(0, 1)
        self.buf[2 + place.y] = self.buf[0] + self.buf[1]
        self.give(1, 2 + place.y, [place.y_peer(d) for d in (4, 3, 5, 2, 6, 1, 7)])

    def over_z(self):
        place = self.place
        self.take(1, NY - 1)
        total = self.buf[2]
        for i in range(1, NY):
            total = total + self.buf[2 + i]
        self.buf[2 + NY + place.high] = total
        self.give(2, 2 + NY + place.high, [place.z_peer(d) for d in (2, 1, 3)])

    def end(self, reverse):
        place = self.place
        self.take(2, NZ - 1)
        row = jnp.zeros((1, NP), F32)
        for base, count, mine in ((0, 2, place.core), (2, NY, place.y), (2 + NY, NZ, place.high)):
            for i in range(count):
                reached = (mine < i) if reverse else (mine > i)
                row = row + self.buf[base + i] * jnp.where(reached, 1.0, 0.0)
        return column(row, NP)[0:NB]


def kernel(*refs):
    (sens_h, demand_h, cost_h, olim_h, gen_h, llim_h, line_h, sbus_h, clim_h, chg_h, lstart_h, llev_h, ldual_h, bal_h) = refs[:14]
    (gen_o, chg_o, level_o, line_o, ldual_o, bal_o) = refs[14:20]
    (sens, demand, cost, olim_r, gen, llim_r, sbus_r, clim_r, chg, lstart_r, llev_r, ldual, bal) = refs[20:33]
    (shi, slo, tail, lines1, lines2, inj1, inj2, cols, chi, clo, piece, acc, pad_l, pad_c, pad_i, hot, hot_t, spread, pre) = refs[33:52]
    (in_sem, g1s, g1r, g2s, g2r, i1s, i1r, i2s, i2r, cbs, cbr, crs, crr, ps, pr) = refs[52:]
    place = Place()
    sends = Sends()

    ins = {}
    for i, (src, dst) in enumerate(
        (
            (line_h, lines1.at[place.bus]),
            (ldual_h, ldual),
            (sens_h, sens),
            (llim_h, llim_r),
            (sbus_h, sbus_r),
            (olim_h, olim_r),
            (clim_h, clim_r),
            (lstart_h, lstart_r),
            (llev_h, llev_r),
            (bal_h, bal),
            (demand_h, demand),
            (cost_h, cost),
            (gen_h, gen),
            (chg_h, chg),
        )
    ):
        ins[i] = pltpu.make_async_copy(src, dst, in_sem.at[i])
        ins[i].start()

    barrier = pltpu.get_barrier_semaphore()
    partners = [place.bus_peer(*d) for d in PEERS]
    partners += [place.core_peer()]
    partners += [place.y_peer(d) for d in range(1, NY)]
    partners += [place.z_peer(d) for d in range(1, NZ)]
    for device in partners:
        pl.semaphore_signal(barrier, inc=1, device_id=device, device_id_type=MESH)

    zeros = jnp.zeros((NP - NB, HD), F32)
    for ref in (pad_l, pad_c, pad_i):
        ref[NB:NP, :] = zeros
    acc[...] = jnp.zeros((NP, HD), F32)
    ins[0].wait()
    pl.semaphore_wait(barrier, len(partners))

    gather1 = Gather(place, sends, lines1, LD, 208, g1s, g1r)
    gather1.begin()
    prefixes = [Prefix(place, sends, pre.at[k], ps.at[k], pr.at[k]) for k in range(4)]
    ins[1].wait()
    pad_l[0:NB, :] = ldual[...]
    prefixes[0].begin(pad_l[...])
    ins[2].wait()
    tail[0:26, :] = sens[224:NB, :]
    tail[26:32, :] = jnp.zeros((6, NL), F32)
    columns = Columns(place, sends, cols, piece, cbs, cbr, crs, crr)
    eighth = columns.eighth()

    @pl.when(eighth < 7)
    def _():
        piece[...] = sens[pl.ds(pl.multiple_of(eighth * PIECE, PIECE), PIECE), :]

    @pl.when(eighth == 7)
    def _():
        piece[...] = tail[...]

    columns.begin()
    prefixes[0].over_y()
    first_line = pl.multiple_of(place.bus * LD, HD)
    cols[0, 0:224, :] = sens[0:224, pl.ds(first_line, LD)]
    cols[0, 224:NP, :] = tail[:, pl.ds(first_line, LD)]

    @pl.loop(0, 14)
    def _(i):
        rows = pl.ds(pl.multiple_of(i * 16, 16), 16)
        shi[rows, :], slo[rows, :] = halves(sens[rows, :])

    shi[224:NP, :], slo[224:NP, :] = halves(tail[...])

    for i in range(3, ARRAYS):
        ins[i].wait()

    olim = column(olim_r[0:1, :], NB)
    clim = column(clim_r[0:1, :], NB)
    lstart = column(lstart_r[0:1, :], NB)
    llev = column(llev_r[0:1, :], NB)
    llim = column(llim_r[0:1, pl.ds(first_line, LD)], LD)
    at_bus = lax.broadcasted_iota(jnp.int32, (NP, NB), 0)
    local = sbus_r[0:1, :] - place.bus * NB
    spread[...] = jnp.zeros((NP, NP), F32)
    spread[:, 0:NB] = (at_bus == local).astype(F32)
    hot[...] = spread[...].astype(BF16)
    hot_t[...] = spread[...].T.astype(BF16)
    hour_at = lax.broadcasted_iota(jnp.int32, (HD, HD), 0)
    hour_to = lax.broadcasted_iota(jnp.int32, (HD, HD), 1)
    until = (hour_at <= hour_to).astype(F32).astype(BF16)
    since = (hour_at >= hour_to).astype(F32).astype(BF16)
    hour_pos = (place.hour * HD + lax.broadcasted_iota(jnp.int32, (1, HD), 1)).astype(F32)
    step = 1.0 / (float(HOURS) - hour_pos + 4.0)

    def add_adjoint(lines):
        def use(block):
            cols = pl.ds(pl.multiple_of(block * LD, HD), LD)
            high, low = halves(lines[block])
            sh = shi[:, cols]
            acc[...] += dot(sh, high, ((1,), (0,))) + (dot(slo[:, cols], high, ((1,), (0,))) + dot(sh, low, ((1,), (0,))))

        return use

    def primal(balance, later, prefix):
        adjoint = acc[0:NB, :]
        at_storage = dot_exact(hot_t[...], acc[...], ((1,), (0,)))[0:NB]
        generation, charging = gen[...], chg[...]
        charge_new = jnp.clip(charging - step * (later - at_storage - balance), -clim, clim)
        pad_c[0:NB, :] = 2.0 * charge_new - charging
        prefix.begin(pad_c[...])
        output_new = jnp.clip(generation - 0.25 * (cost[...] + adjoint + balance), 0.0, olim)
        gen[...] = output_new
        chg[...] = charge_new
        return 2.0 * output_new - generation - demand[...]

    def inject(output_bar, buf, send_sem, recv_sem, prefix):
        pad_i[0:NB, :] = output_bar - dot_exact(hot[...], pad_c[...], ((1,), (0,)))[0:NB]
        prefix.over_y()
        buf[place.bus] = pad_i[...].T
        gather = Gather(place, sends, buf, HD, 72, send_sem, recv_sem)
        gather.begin()
        return gather

    def split_columns():
        for k in range(8):
            chi[k], clo[k] = halves(cols[k])

    def flows_of(gather, buf, beside):
        sums = [jnp.zeros((HD, LD), F32), jnp.zeros((HD, NP), F32)]

        def use(block):
            k = lax.rem(block - place.bus + 8, 8)
            injection = buf[block]
            high, low = halves(injection)
            ch = chi[k]
            sums[0] += dot(high, ch, ((1,), (0,))) + (dot(low, ch, ((1,), (0,))) + dot(high, clo[k], ((1,), (0,))))
            sums[1] += injection

        gather.run(use, beside)
        total = dot(jnp.ones((ROW, NP), F32), sums[1], ((1,), (1,)), HIGHEST)
        return sums[0].T, total[0:1]

    def line_step(line, flows):
        raised = 4.0 * line + flows
        return 0.25 * (raised - jnp.clip(raised, -llim, llim))

    def level_step(carried):
        level = lstart + carried + dot_exact(pad_c[...], until, ((1,), (0,)))[0:NB]
        raised = 4.0 * pad_l[0:NB, :] + level
        pad_l[0:NB, :] = 0.25 * (raised - jnp.clip(raised, 0.0, llev))
        return level

    def later_of(carried):
        return carried + dot_exact(pad_l[...], since, ((1,), (0,)))[0:NB]

    def beside(at):
        if at == 2:
            prefixes[0].over_z()
            columns.fetched()
        if at == 5:
            columns.first_halves()

    gather1.run(add_adjoint(lines1), beside)
    balance = bal[0:1, :]
    output_bar = primal(balance, later_of(prefixes[0].end(True)), prefixes[1])
    gather = inject(output_bar, inj1, i1s, i1r, prefixes[1])
    columns.second_halves()

    def beside(at):
        if at == 1:
            columns.far_halves()
        if at == 2:
            prefixes[1].over_z()
            columns.end()
            split_columns()

    flows, total = flows_of(gather, inj1, beside)
    lines2[place.bus] = line_step(lines1[place.bus], flows)
    gather2 = Gather(place, sends, lines2, LD, 208, g2s, g2r)
    gather2.begin()
    balance = balance + total * (1.0 / float(B + S))
    level_step(prefixes[1].end(False))
    prefixes[2].begin(pad_l[...])
    acc[...] = jnp.zeros((NP, HD), F32)
    prefixes[2].over_y()

    def beside(at):
        if at == 3:
            prefixes[2].over_z()

    gather2.run(add_adjoint(lines2), beside)
    output_bar = primal(balance, later_of(prefixes[2].end(True)), prefixes[3])
    gather = inject(output_bar, inj2, i2s, i2r, prefixes[3])
    gen_o[...] = gen[...]
    chg_o[...] = chg[...]
    flows, total = flows_of(gather, inj2, lambda at: prefixes[3].over_z() if at == 2 else None)
    line_o[...] = line_step(lines2[place.bus], flows)
    bal_o[...] = balance + total * (1.0 / float(B + S))
    level_o[...] = level_step(prefixes[3].end(False))
    ldual_o[...] = pad_l[0:NB, :]
    sends.finish()


def store(*refs):
    copies = [pltpu.make_async_copy(refs[i], refs[6 + i], refs[12].at[i]) for i in range(6)]
    for copy in copies:
        copy.start()
    for copy in copies:
        copy.wait()


def body(
    line_sensitivity,
    demand,
    unit_cost,
    output_limit,
    output_start,
    line_limit,
    line_dual,
    storage_bus,
    charge_limit,
    charge_start,
    level_start,
    level_limit,
    level_dual,
    balance_dual,
):
    anywhere = pl.BlockSpec(memory_space=pl.ANY)
    block = jax.ShapeDtypeStruct((NB, HD), F32)
    vm = pltpu.VMEM
    dma = pltpu.SemaphoreType.DMA
    scratch = [
        vm((NB, NL), F32),
        vm((NB, HD), F32),
        vm((NB, HD), F32),
        vm((1, NB), F32),
        vm((NB, HD), F32),
        vm((1, NL), F32),
        vm((1, NB), jnp.int32),
        vm((1, NB), F32),
        vm((NB, HD), F32),
        vm((1, NB), F32),
        vm((1, NB), F32),
        vm((NB, HD), F32),
        vm((1, HD), F32),
        vm((NP, NL), BF16),
        vm((NP, NL), BF16),
        vm((PIECE, NL), F32),
        vm((8, LD, HD), F32),
        vm((8, LD, HD), F32),
        vm((8, HD, NP), F32),
        vm((8, HD, NP), F32),
        vm((8, NP, LD), F32),
        vm((8, NP, LD), BF16),
        vm((8, NP, LD), BF16),
        vm((PIECE, NL), F32),
        vm((NP, HD), F32),
        vm((NP, HD), F32),
        vm((NP, HD), F32),
        vm((NP, HD), F32),
        vm((NP, NP), BF16),
        vm((NP, NP), BF16),
        vm((NP, NP), F32),
        vm((4, Prefix.SLOTS, 1, NP), F32),
        dma((ARRAYS,)),
        dma,
        dma((16,)),
        dma,
        dma((16,)),
        dma,
        dma((16,)),
        dma,
        dma((16,)),
        dma,
        dma,
        dma,
        dma((10,)),
        dma((4, 3)),
        dma((4, 3)),
    ]
    shapes = (block, block, block, jax.ShapeDtypeStruct((LD, HD), F32), block, jax.ShapeDtypeStruct((1, HD), F32))
    results = pl.pallas_call(
        kernel,
        out_shape=tuple(pltpu.VMEM(shape.shape, F32) for shape in shapes),
        in_specs=[anywhere] * ARRAYS,
        out_specs=[pl.BlockSpec(memory_space=pltpu.VMEM)] * 6,
        scratch_shapes=scratch,
        compiler_params=pltpu.CompilerParams(collective_id=0, has_side_effects=True, vmem_limit_bytes=56 * 1024 * 1024),
    )(
        line_sensitivity,
        demand,
        unit_cost,
        output_limit.reshape(1, NB),
        output_start,
        line_limit.reshape(1, NL),
        line_dual,
        storage_bus.reshape(1, NB),
        charge_limit.reshape(1, NB),
        charge_start,
        level_start.reshape(1, NB),
        level_limit.reshape(1, NB),
        level_dual,
        balance_dual.reshape(1, HD),
    )
    generation, charging, level, line, dual, balance = pl.pallas_call(
        store,
        out_shape=shapes,
        in_specs=[anywhere] * 6,
        out_specs=[anywhere] * 6,
        scratch_shapes=[dma((6,))],
        compiler_params=pltpu.CompilerParams(vmem_limit_bytes=32 * 1024 * 1024),
    )(*[pltpu.with_memory_space_constraint(result, pltpu.VMEM) for result in results])
    return generation, charging, level, line, dual, balance.reshape(HD)


def solution(mesh):
    both = P("bus", "hour")
    return jax.shard_map(
        body,
        mesh=mesh,
        in_specs=(
            P("bus", None),
            both,
            both,
            P("bus"),
            both,
            P(),
            both,
            P("bus"),
            P("bus"),
            both,
            P("bus"),
            P("bus"),
            both,
            P("hour"),
        ),
        out_specs=(both, both, both, both, both, P("hour")),
        check_vma=False,
    )
```
